128 devices in a mesh: tm: 4 (over z_hi, core), rows: 4 (over y), heads: 8 (over z_lo, x).
Axes of the slice: x: 4, y: 4, z: 4 (z_hi: 2, z_lo: 2; z = z_hi * 2 + z_lo), core: 2. Of those that a mesh axis runs over, the one named last changes fastest.
Arguments:
- queries: bfloat16 [4, 4, 3, 8, 256, 128], P('tm', 'rows', None, 'heads'), parts along dimension 3, may hold values from -8 to 8
- keys: bfloat16 [4, 4, 3, 8, 256, 128], P('tm', 'rows', None, 'heads'), parts along dimension 3, may hold values from -8 to 8
- values: bfloat16 [4, 4, 3, 8, 256, 128], P('tm', 'rows', None, 'heads'), parts along dimension 3, may hold values from -6 to 6
- d_out: bfloat16 [4, 4, 3, 8, 256, 128], P('tm', 'rows', None, 'heads'), parts along dimension 3, may hold values from -6 to 6
- window_mask: int32 [4, 4, 3, 8, 27], P('tm', 'rows', None, 'heads'), parts along dimension 3, may hold values from 0 to 1, as said below
Outputs:
- attended: bfloat16 [4, 4, 3, 8, 256, 128], P('tm', 'rows', None, 'heads'), parts along dimension 3
- grad_q: bfloat16 [4, 4, 3, 8, 256, 128], P('tm', 'rows', None, 'heads'), parts along dimension 3
- grad_k: bfloat16 [4, 4, 3, 8, 256, 128], P('tm', 'rows', None, 'heads'), parts along dimension 3
- grad_v: bfloat16 [4, 4, 3, 8, 256, 128], P('tm', 'rows', None, 'heads'), parts along dimension 3
The draws below stay inside these ranges and needn't reach their ends.
There are 8 independent parts, one for each index of `heads`. The reference program is written for one: setup_inputs(seed, part) draws one part's arguments, and reference() takes and returns one part's arrays. A program takes and returns all parts, laid end to end along the dimension named above; each array names one. Nothing has to cross between parts.
Inputs may be any that keep to these rules, and one draw needn't show every extreme that they name: `window_mask`: an entry is 0 wherever the offset tile lies outside the grid, the centre entry (index 13) is always 1, and the mask is symmetric: the entry of tile g at offset o equals the entry of tile g + o at offset -o.
All inputs are finite; a program needn't handle non-finite values.
Results may differ from the reference program's by a relative error of at most 0.013.
Values may be sent and summed in bfloat16 or wider, within the bound.
No kernel may reach another device: no remote copies, remote signals or barrier semaphores. Data moves between devices by JAX's collectives and lax.ppermute only.
A program may use at most 64 MiB of HBM per device.

```python
import jax
import jax.numpy as jnp
from jax import lax

HD = 128
TC = 3
HEADS_DEV = 1
TILE = 256
TT = 4
TR = 4


def grid_shape():
    return (TT, TR, TC, HEADS_DEV, TILE, HD)


def draw_queries(key, part):
    own = jax.random.fold_in(key, 11)
    return (1.6 * jax.random.truncated_normal(own, -4.5, 4.5, grid_shape(), jnp.float32)).astype(jnp.bfloat16)


def draw_keys(key, part):
    own = jax.random.fold_in(key, 23)
    return (1.6 * jax.random.truncated_normal(own, -4.5, 4.5, grid_shape(), jnp.float32)).astype(jnp.bfloat16)


def draw_window_mask(key, part):
    own = jax.random.fold_in(key, 37)
    dense = jax.random.randint(jax.random.fold_in(own, 1), (TT, TR, TC, HEADS_DEV, 1), 0, 4) == 0
    limit = jnp.where(dense, 14, 6)
    bits = (jax.random.randint(jax.random.fold_in(own, 2), (TT, TR, TC, HEADS_DEV, 27), 0, 16) < limit).astype(jnp.int32)
    padded = jnp.pad(bits, ((1, 1), (1, 1), (1, 1), (0, 0), (0, 0)))
    frame = jnp.arange(TT, dtype=jnp.int32)[:, None, None, None]
    row = jnp.arange(TR, dtype=jnp.int32)[None, :, None, None]
    column = jnp.arange(TC, dtype=jnp.int32)[None, None, :, None]
    columns = []
    for offset in range(27):
        step_t = offset // 9 - 1
        step_r = offset // 3 % 3 - 1
        step_c = offset % 3 - 1
        inside = (frame + step_t >= 0) & (frame + step_t < TT) & (row + step_r >= 0) & (row + step_r < TR)
        inside = inside & (column + step_c >= 0) & (column + step_c < TC)
        if offset > 13:
            entry = bits[..., offset]
        elif offset == 13:
            entry = jnp.ones((TT, TR, TC, HEADS_DEV), jnp.int32)
        else:
            entry = padded[1 + step_t:1 + step_t + TT, 1 + step_r:1 + step_r + TR, 1 + step_c:1 + step_c + TC, :, 26 - offset]
        columns.append(entry * inside.astype(jnp.int32))
    return jnp.stack(columns, -1)


def steps_of(own_key, dims, pieces, low, high):
    loudness, own = 1.0, jax.random.fold_in(own_key, 6)
    for position, parts in pieces:
        heights = jnp.exp(jax.random.uniform(jax.random.fold_in(own, position), (parts,), jnp.float32, low / len(pieces), high / len(pieces)))
        loudness = loudness * jnp.repeat(heights, dims[position] // parts).reshape([-1 if axis == position else 1 for axis in range(len(dims))])
    return loudness


def centred(stream_key, extent, spread, most, cuts=(), kind=jnp.bfloat16):
    drawn = jax.random.normal(stream_key, extent, jnp.float32) * spread
    if len(cuts) > 0:
        drawn = steps_of(stream_key, extent, cuts, -0.22, 0.18) * drawn
    return jnp.clip(drawn, min=-most, max=most).astype(kind)


def setup_inputs(seed: int = 0, part: int = 0) -> dict:
    seeds = jax.random.split(jax.random.key(seed), 6)
    part_splits = jax.random.split(jax.random.fold_in(seeds[5], part), 6)
    queries = draw_queries(jax.random.fold_in(jax.random.fold_in(seeds[5], part), 71), part)
    keys = draw_keys(jax.random.fold_in(jax.random.fold_in(seeds[5], part), 71), part)
    values = centred(part_splits[2], (TT, TR, TC, HEADS_DEV, TILE, HD), 1.0, 6.0, ((0, 4), (1, 4)))
    d_out = centred(part_splits[3], (TT, TR, TC, HEADS_DEV, TILE, HD), 1.0, 6.0, ((0, 4), (1, 4)))
    window_mask = draw_window_mask(jax.random.fold_in(jax.random.fold_in(seeds[5], part), 71), part)
    return dict(queries=queries, keys=keys, values=values, d_out=d_out, window_mask=window_mask)


def pad_grid(field):
    return jnp.pad(field, [(1, 1), (1, 1), (1, 1)] + [(0, 0)] * (field.ndim - 3))


def window_of(padded, place):
    zero = jnp.int32(0)
    start = (place[0], place[1], place[2]) + (zero,) * (padded.ndim - 3)
    block = lax.dynamic_slice(padded, start, (3, 3, 3) + padded.shape[3:])
    return block.reshape((27,) + padded.shape[3:])


def flat_tiles(block):
    moved = jnp.moveaxis(block, 0, 1)
    return moved.reshape((moved.shape[0], moved.shape[1] * moved.shape[2]) + moved.shape[3:])


def place_of(index):
    return (index // (TR * TC), (index // TC) % TR, index % TC)


def reference(queries, keys, values, d_out, window_mask):
    scale = HD ** -0.5
    order = jnp.arange(TT * TR * TC, dtype=jnp.int32)
    key_pad = pad_grid(keys)
    value_pad = pad_grid(values)

    def forward_tile(index):
        place = place_of(index)
        query = queries[place].astype(jnp.float32)
        near_k = flat_tiles(window_of(key_pad, place)).astype(jnp.float32)
        near_v = flat_tiles(window_of(value_pad, place)).astype(jnp.float32)
        keep = jnp.repeat(window_mask[place], TILE, axis=1) > 0
        scores = jnp.einsum("hid,hjd->hij", query, near_k) * scale
        scores = jnp.where(keep[:, None, :], scores, -jnp.inf)
        top = jnp.max(scores, -1, keepdims=True)
        log_total = top[..., 0] + jnp.log(jnp.sum(jnp.exp(scores - top), -1))
        weights = jnp.exp(scores - log_total[..., None]).astype(jnp.bfloat16)
        attended = jnp.einsum("hij,hjd->hid", weights.astype(jnp.float32), near_v)
        return attended.astype(jnp.bfloat16), log_total

    attended, log_total = lax.map(forward_tile, order)
    attended = attended.reshape(queries.shape)
    log_total = log_total.reshape(queries.shape[:-1])
    delta = jnp.sum(d_out.astype(jnp.float32) * attended.astype(jnp.float32), -1)

    def query_tile(index):
        place = place_of(index)
        query = queries[place].astype(jnp.float32)
        grad_out = d_out[place].astype(jnp.float32)
        near_k = flat_tiles(window_of(key_pad, place)).astype(jnp.float32)
        near_v = flat_tiles(window_of(value_pad, place)).astype(jnp.float32)
        keep = jnp.repeat(window_mask[place], TILE, axis=1) > 0
        scores = jnp.einsum("hid,hjd->hij", query, near_k) * scale
        scores = jnp.where(keep[:, None, :], scores, -jnp.inf)
        probs = jnp.exp(scores - log_total[place][..., None])
        grad_w = jnp.einsum("hid,hjd->hij", grad_out, near_v)
        grad_s = (probs * (grad_w - delta[place][..., None])).astype(jnp.bfloat16)
        grad_q = scale * jnp.einsum("hij,hjd->hid", grad_s.astype(jnp.float32), near_k)
        return grad_q.astype(jnp.bfloat16)

    grad_q = lax.map(query_tile, order).reshape(queries.shape)

    query_pad = pad_grid(queries)
    grad_pad = pad_grid(d_out)
    log_pad = pad_grid(log_total)
    delta_pad = pad_grid(delta)
    mask_pad = pad_grid(window_mask)
    positions = jnp.arange(27, dtype=jnp.int32)
    opposite = 26 - positions

    def key_tile(index):
        place = place_of(index)
        own_k = keys[place].astype(jnp.float32)
        own_v = values[place].astype(jnp.float32)
        near_q = flat_tiles(window_of(query_pad, place)).astype(jnp.float32)
        near_g = flat_tiles(window_of(grad_pad, place)).astype(jnp.float32)
        near_log = flat_tiles(window_of(log_pad, place))
        near_delta = flat_tiles(window_of(delta_pad, place))
        masks = window_of(mask_pad, place)
        chosen = masks[positions, :, opposite]
        keep = jnp.repeat(jnp.transpose(chosen), TILE, axis=1) > 0
        scores = jnp.einsum("hid,hjd->hij", near_q, own_k) * scale
        scores = jnp.where(keep[:, :, None], scores, -jnp.inf)
        probs = jnp.exp(scores - near_log[..., None])
        weights = probs.astype(jnp.bfloat16)
        grad_v = jnp.einsum("hij,hid->hjd", weights.astype(jnp.float32), near_g)
        grad_w = jnp.einsum("hid,hjd->hij", near_g, own_v)
        grad_s = (probs * (grad_w - near_delta[..., None])).astype(jnp.bfloat16)
        grad_k = scale * jnp.einsum("hij,hid->hjd", grad_s.astype(jnp.float32), near_q)
        return grad_k.astype(jnp.bfloat16), grad_v.astype(jnp.bfloat16)

    grad_k, grad_v = lax.map(key_tile, order)
    return attended, grad_q, grad_k.reshape(keys.shape), grad_v.reshape(values.shape)
```

```python
import math

import jax
import jax.numpy as jnp
from jax import lax
from jax.experimental import pallas as pl
from jax.experimental.pallas import tpu as pltpu
from jax.sharding import PartitionSpec as P

TM, ROWS = "tm", "rows"
F32, BF16 = jnp.float32, jnp.bfloat16
SLOTS = 9
ROW_STEPS = (0, -1, 1)
NT = (((1,), (1,)), ((), ()))
NN = (((1,), (0,)), ((), ()))


def dot(left, right, dims):
    return lax.dot_general(left, right, dims, preferred_element_type=F32)


def find_pairs(mask, pairs, counts, columns):
    near = 1 - 2 * lax.rem(lax.axis_index(TM), 2)
    frame_steps = (0, near, -near)
    for c in range(columns):
        n = jnp.int32(0)
        for slot in range(SLOTS):
            dt, dr = frame_steps[slot // 3], ROW_STEPS[slot % 3]
            for other in range(max(c - 1, 0), min(c + 2, columns)):
                pairs[c * 27 + n] = slot * columns + other
                n = n + mask[c, 9 * (dt + 1) + 3 * (dr + 1) + other - c + 1]
        counts[c] = n


def pack_kernel(q, k, v, g, kv, qg):
    kv[0], kv[1], qg[0], qg[1] = k[...], v[...], q[...], g[...]


def query_kernel(columns, tile, scale, mask, own, *refs):
    slots, (out, grad_q, stats) = refs[:SLOTS], refs[SLOTS:SLOTS + 3]
    near, mine, s_all, w_all, top, low, acc, pairs, counts, sems = refs[SLOTS + 3:]
    copies = [pltpu.make_async_copy(own, mine, sems.at[SLOTS])]
    copies += [pltpu.make_async_copy(slots[s], near.at[s], sems.at[s]) for s in range(SLOTS)]
    for copy in copies:
        copy.start()
    find_pairs(mask, pairs, counts, columns)
    for copy in copies:
        copy.wait()
    unit = scale * math.log2(math.e)

    def key_tile(which, entry):
        slot, column = entry // columns, lax.rem(entry, columns)
        return near[slot, which, pl.ds(pl.multiple_of(column * tile, tile), tile), :]

    for c in range(columns):
        rows = slice(c * tile, (c + 1) * tile)
        q = mine[0, rows, :]
        g = mine[1, rows, :]
        n = counts[c]
        top[...] = jnp.full(top.shape, -jnp.inf, F32)

        def score_step(i, carry):
            s = dot(q, key_tile(0, pairs[c * 27 + i]), NT) * unit
            s_all[i] = s
            top[...] = jnp.maximum(top[...], jnp.maximum(s[:, :128], s[:, 128:]))
            return carry

        lax.fori_loop(0, n, score_step, 0)
        peak = jnp.max(top[...], axis=1, keepdims=True)
        top[...] = jnp.broadcast_to(peak, top.shape)
        low[...] = jnp.zeros(low.shape, F32)
        acc[...] = jnp.zeros(acc.shape, F32)

        def value_step(i, carry):
            v = key_tile(1, pairs[c * 27 + i])
            m = top[...]
            e = jnp.exp2(s_all[i] - jnp.concatenate([m, m], 1))
            s_all[i] = e
            low[...] += e[:, :128] + e[:, 128:]
            acc[...] += dot(e.astype(BF16), v, NN)
            w_all[i] = dot(g, v, NT)
            return carry

        lax.fori_loop(0, n, value_step, 0)
        total = jnp.sum(low[...], axis=1, keepdims=True)
        inverse = 1.0 / total
        attended = (acc[...] * inverse).astype(BF16)
        out[rows, :] = attended
        delta = jnp.sum(g.astype(F32) * attended.astype(F32), axis=1, keepdims=True)
        top[...] = jnp.broadcast_to(delta, top.shape)
        acc[...] = jnp.zeros(acc.shape, F32)

        def query_step(i, carry):
            d = top[...]
            ds = s_all[i] * (w_all[i] - jnp.concatenate([d, d], 1))
            acc[...] += dot(ds.astype(BF16), key_tile(0, pairs[c * 27 + i]), NN)
            return carry

        lax.fori_loop(0, n, query_step, 0)
        grad_q[rows, :] = (acc[...] * (inverse * scale)).astype(BF16)
        log_total = peak + jnp.log2(total)
        lane = lax.broadcasted_iota(jnp.int32, (tile, 128), 1)
        both = jnp.where(lane == 0, log_total, delta).T
        stats[c:c + 1, :] = both[0:1]
        stats[4 + c:5 + c, :] = both[1:2]


def key_kernel(columns, tile, scale, mask, own, *refs):
    slots, slot_stats = refs[:SLOTS], refs[SLOTS:2 * SLOTS]
    grad_k, grad_v = refs[2 * SLOTS:2 * SLOTS + 2]
    near, mine, stat, k_acc, v_acc, pairs, counts, sems = refs[2 * SLOTS + 2:]
    copies = [pltpu.make_async_copy(own, mine, sems.at[2 * SLOTS])]
    for s in range(SLOTS):
        copies.append(pltpu.make_async_copy(slots[s], near.at[s], sems.at[s]))
        copies.append(pltpu.make_async_copy(slot_stats[s], stat.at[s], sems.at[SLOTS + s]))
    for copy in copies:
        copy.start()
    find_pairs(mask, pairs, counts, columns)
    for copy in copies:
        copy.wait()
    unit = scale * math.log2(math.e)
    for c in range(columns):
        rows = slice(c * tile, (c + 1) * tile)
        k = mine[0, rows, :]
        v = mine[1, rows, :]
        k_acc[...] = jnp.zeros(k_acc.shape, F32)
        v_acc[...] = jnp.zeros(v_acc.shape, F32)

        def step(i, carry):
            entry = pairs[c * 27 + i]
            slot, column = entry // columns, lax.rem(entry, columns)
            at = pl.ds(pl.multiple_of(column * tile, tile), tile)
            q, g = near[slot, 0, at, :], near[slot, 1, at, :]
            log_total = stat[slot, pl.ds(column, 1), :]
            delta = stat[slot, pl.ds(4 + column, 1), :]
            p = jnp.exp2(dot(k, q, NT) * unit - log_total)
            v_acc[...] += dot(p.astype(BF16), g, NN)
            ds = p * (dot(v, g, NT) - delta)
            k_acc[...] += dot(ds.astype(BF16), q, NN)
            return carry

        lax.fori_loop(0, counts[c], step, 0)
        grad_k[rows, :] = (k_acc[...] * scale).astype(BF16)
        grad_v[rows, :] = v_acc[...].astype(BF16)


def ring(axis, step):
    count = lax.axis_size(axis)
    return [(i, (i + step) % count) for i in range(count)]


def pair_up(axis, first):
    count = lax.axis_size(axis)
    to = list(range(count))
    for i in range(first, count - 1, 2):
        to[i], to[i + 1] = i + 1, i
    return list(enumerate(to))


def spread(x):
    before, after = ring(ROWS, 1), ring(ROWS, -1)
    near, far = pair_up(TM, 0), pair_up(TM, 1)
    up = lax.ppermute(x, ROWS, before)
    down = lax.ppermute(x, ROWS, after)
    other = lax.ppermute(x, TM, near)
    z = lax.ppermute(x, TM, far)
    return [
        x, up, down,
        other, lax.ppermute(up, TM, near), lax.ppermute(down, TM, near),
        z, lax.ppermute(z, ROWS, before), lax.ppermute(z, ROWS, after),
    ]


ANY = pl.BlockSpec(memory_space=pl.ANY)
VMEM = pl.BlockSpec(memory_space=pltpu.VMEM)
SMEM = pl.BlockSpec(memory_space=pltpu.SMEM)


def body(queries, keys, values, d_out, window_mask):
    columns, tile, width = queries.shape[2], queries.shape[4], queries.shape[5]
    tokens = columns * tile
    scale = width ** -0.5
    flat = lambda x: x.reshape(tokens, width)
    mask = window_mask.reshape(columns, 27)
    pair = jax.ShapeDtypeStruct((2, tokens, width), BF16)
    field = jax.ShapeDtypeStruct((tokens, width), BF16)
    kv, qg = pl.pallas_call(
        pack_kernel,
        out_shape=(pair, pair),
        in_specs=[VMEM] * 4,
        out_specs=(VMEM, VMEM),
        name="pack",
    )(flat(queries), flat(keys), flat(values), flat(d_out))
    near_kv = spread(kv)
    near_qg = spread(qg)
    params = pltpu.CompilerParams(vmem_limit_bytes=40 * 2**20)
    lists = [
        pltpu.SMEM((columns * 27 + 1,), jnp.int32),
        pltpu.SMEM((columns,), jnp.int32),
    ]
    total = pltpu.VMEM((tile, width), F32)
    attended, grad_q, stats = pl.pallas_call(
        lambda *refs: query_kernel(columns, tile, scale, *refs),
        out_shape=(field, field, jax.ShapeDtypeStruct((8, tile), F32)),
        in_specs=[SMEM, ANY] + [ANY] * SLOTS,
        out_specs=(VMEM, VMEM, VMEM),
        scratch_shapes=[
            pltpu.VMEM((SLOTS, 2, tokens, width), BF16),
            pltpu.VMEM((2, tokens, width), BF16),
            pltpu.VMEM((27, tile, tile), F32),
            pltpu.VMEM((27, tile, tile), F32),
            total, total, total,
            *lists,
            pltpu.SemaphoreType.DMA((SLOTS + 1,)),
        ],
        compiler_params=params,
        cost_estimate=pl.CostEstimate(
            flops=32 * 5 * 2 * tile * tile * width, bytes_accessed=8 * tokens * width, transcendentals=32 * tile * tile
        ),
        name="query_side",
    )(mask, qg, *near_kv)
    near_stats = spread(stats)
    grad_k, grad_v = pl.pallas_call(
        lambda *refs: key_kernel(columns, tile, scale, *refs),
        out_shape=(field, field),
        in_specs=[SMEM, ANY] + [ANY] * (2 * SLOTS),
        out_specs=(VMEM, VMEM),
        scratch_shapes=[
            pltpu.VMEM((SLOTS, 2, tokens, width), BF16),
            pltpu.VMEM((2, tokens, width), BF16),
            pltpu.VMEM((SLOTS, 8, tile), F32),
            total, total,
            *lists,
            pltpu.SemaphoreType.DMA((2 * SLOTS + 1,)),
        ],
        compiler_params=params,
        cost_estimate=pl.CostEstimate(
            flops=32 * 4 * 2 * tile * tile * width, bytes_accessed=8 * tokens * width, transcendentals=32 * tile * tile
        ),
        name="key_side",
    )(mask, kv, *near_qg, *near_stats)
    return tuple(x.reshape(queries.shape) for x in (attended, grad_q, grad_k, grad_v))


def solution(mesh):
    field = P(TM, ROWS, None, "heads", None, None)
    return jax.shard_map(
        body,
        mesh=mesh,
        in_specs=(field, field, field, field, P(TM, ROWS, None, "heads", None)),
        out_specs=(field, field, field, field),
        check_vma=False,
    )
```

```python
import math

import jax
import jax.numpy as jnp
from jax import lax
from jax.experimental import pallas as pl
from jax.experimental.pallas import tpu as pltpu
from jax.sharding import PartitionSpec as P

TM, ROWS = "tm", "rows"
F32, BF16 = jnp.float32, jnp.bfloat16
SLOTS = 9
LIST = 32
GQ = 4
GK = 4
DP = 2
ROW_STEPS = (0, -1, 1)
NT = (((1,), (1,)), ((), ()))
NN = (((1,), (0,)), ((), ()))


def dot(left, right, dims):
    return lax.dot_general(left, right, dims, preferred_element_type=F32)


def find_pairs(mask, pairs, counts, columns, group):
    near = 1 - 2 * lax.rem(lax.axis_index(TM), 2)
    frame_steps = (0, near, -near)
    for c in range(columns):
        n = jnp.int32(0)
        for slot in range(SLOTS):
            dt, dr = frame_steps[slot // 3], ROW_STEPS[slot % 3]
            for other in range(max(c - 1, 0), min(c + 2, columns)):
                pairs[c * LIST + n] = slot * columns + other
                n = n + mask[c, 9 * (dt + 1) + 3 * (dr + 1) + other - c + 1]
        counts[c] = n
        for extra in range(group - 1):
            pairs[c * LIST + n + extra] = c


def pack_kernel(q, k, v, g, kv, qg):
    kv[0], kv[1], qg[0], qg[1] = k[...], v[...], q[...], g[...]


def query_kernel(columns, tile, scale, mask, own, *refs):
    slots, (out, grad_q, stats) = refs[:SLOTS], refs[SLOTS:SLOTS + 3]
    near, mine, s_all, w_all, top, low, acc, pairs, counts, sems = refs[SLOTS + 3:]
    copies = [pltpu.make_async_copy(own, mine, sems.at[SLOTS])]
    copies += [pltpu.make_async_copy(slots[s], near.at[s], sems.at[s]) for s in range(SLOTS)]
    for copy in copies:
        copy.start()
    find_pairs(mask, pairs, counts, columns, GQ)
    for copy in copies:
        copy.wait()
    unit = scale * math.log2(math.e)

    def key_tile(which, entry):
        slot, column = entry // columns, lax.rem(entry, columns)
        return near[slot, which, pl.ds(pl.multiple_of(column * tile, tile), tile), :]

    def wide(x):
        return jnp.concatenate([x, x], 1)

    for c in range(columns):
        rows = slice(c * tile, (c + 1) * tile)
        n = counts[c]
        steps = (n + GQ - 1) // GQ
        top[...] = jnp.full(top.shape, -jnp.inf, F32)

        def entries(i):
            return [pairs[c * LIST + GQ * i + j] for j in range(GQ)]

        def score_step(i, carry):
            q = mine[0, rows, :]
            best = top[...]
            for j, entry in enumerate(entries(i)):
                s = dot(q, key_tile(0, entry), NT) * unit
                s_all[GQ * i + j] = s
                best = jnp.maximum(best, jnp.maximum(s[:, :128], s[:, 128:]))
            top[...] = best
            if DP == 1:
                g = mine[1, rows, :]
                for j, entry in enumerate(entries(i)):
                    w_all[GQ * i + j] = dot(g, key_tile(1, entry), NT)
            return carry

        lax.fori_loop(0, steps, score_step, 0)
        for j in range(GQ - 1):
            @pl.when(n + j < steps * GQ)
            def _():
                s_all[n + j] = jnp.full((tile, tile), -jnp.inf, F32)
        peak = jnp.max(top[...], axis=1, keepdims=True)
        top[...] = jnp.broadcast_to(peak, top.shape)
        low[...] = jnp.zeros(low.shape, F32)
        acc[...] = jnp.zeros(acc.shape, F32)

        def value_step(i, carry):
            m = wide(top[...])
            l = low[...]
            total = acc[...]
            for j, entry in enumerate(entries(i)):
                v = key_tile(1, entry)
                e = jnp.exp2(s_all[GQ * i + j] - m)
                s_all[GQ * i + j] = e
                l = l + (e[:, :128] + e[:, 128:])
                total = total + dot(e.astype(BF16), v, NN)
            low[...] = l
            acc[...] = total
            if DP == 2:
                g = mine[1, rows, :]
                for j, entry in enumerate(entries(i)):
                    w_all[GQ * i + j] = dot(g, key_tile(1, entry), NT)
            return carry

        lax.fori_loop(0, steps, value_step, 0)
        total = jnp.sum(low[...], axis=1, keepdims=True)
        inverse = 1.0 / total
        attended = (acc[...] * inverse).astype(BF16)
        out[rows, :] = attended
        delta = jnp.sum(mine[1, rows, :].astype(F32) * attended.astype(F32), axis=1, keepdims=True)
        top[...] = jnp.broadcast_to(delta, top.shape)
        acc[...] = jnp.zeros(acc.shape, F32)

        def query_step(i, carry):
            d = wide(top[...])
            sum_q = acc[...]
            for j, entry in enumerate(entries(i)):
                w = dot(mine[1, rows, :], key_tile(1, entry), NT) if DP == 3 else w_all[GQ * i + j]
                ds = s_all[GQ * i + j] * (w - d)
                sum_q = sum_q + dot(ds.astype(BF16), key_tile(0, entry), NN)
            acc[...] = sum_q
            return carry

        lax.fori_loop(0, steps, query_step, 0)
        grad_q[rows, :] = (acc[...] * (inverse * scale)).astype(BF16)
        log_total = peak + jnp.log2(total)
        lane = lax.broadcasted_iota(jnp.int32, (tile, 128), 1)
        both = jnp.where(lane == 0, log_total, delta).T
        stats[c:c + 1, :] = both[0:1]
        stats[4 + c:5 + c, :] = both[1:2]


def key_kernel(columns, tile, scale, mask, own, *refs):
    slots, sets = refs[:SLOTS], refs[SLOTS:SLOTS + 3]
    grad_k, grad_v = refs[SLOTS + 3:SLOTS + 5]
    near, mine, stat, k_acc, v_acc, pairs, counts, sems = refs[SLOTS + 5:]
    copies = [pltpu.make_async_copy(own, mine, sems.at[SLOTS])]
    copies += [pltpu.make_async_copy(slots[s], near.at[s], sems.at[s]) for s in range(SLOTS)]
    for copy in copies:
        copy.start()
    find_pairs(mask, pairs, counts, columns, GK)
    for row in range(3):
        for frame in range(3):
            stat[3 * frame + row] = sets[row][8 * frame:8 * frame + 8, :]
    stat[SLOTS] = jnp.full((8, tile), 1e30, F32)
    for copy in copies:
        copy.wait()
    unit = scale * math.log2(math.e)
    for c in range(columns):
        rows = slice(c * tile, (c + 1) * tile)
        n = counts[c]
        k_acc[...] = jnp.zeros(k_acc.shape, F32)
        v_acc[...] = jnp.zeros(v_acc.shape, F32)

        def step(i, carry):
            k = mine[0, rows, :]
            v = mine[1, rows, :]
            sum_v = v_acc[...]
            sum_k = k_acc[...]
            for j in range(GK):
                entry = pairs[c * LIST + GK * i + j]
                slot, column = entry // columns, lax.rem(entry, columns)
                at = pl.ds(pl.multiple_of(column * tile, tile), tile)
                q, g = near[slot, 0, at, :], near[slot, 1, at, :]
                held = jnp.where(GK * i + j < n, slot, SLOTS)
                log_total = stat[held, pl.ds(column, 1), :]
                delta = stat[slot, pl.ds(4 + column, 1), :]
                p = jnp.exp2(dot(k, q, NT) * unit - log_total)
                sum_v = sum_v + dot(p.astype(BF16), g, NN)
                ds = p * (dot(v, g, NT) - delta)
                sum_k = sum_k + dot(ds.astype(BF16), q, NN)
            v_acc[...] = sum_v
            k_acc[...] = sum_k
            return carry

        lax.fori_loop(0, (n + GK - 1) // GK, step, 0)
        grad_k[rows, :] = (k_acc[...] * scale).astype(BF16)
        grad_v[rows, :] = v_acc[...].astype(BF16)


def ring(axis, step):
    count = lax.axis_size(axis)
    return [(i, (i + step) % count) for i in range(count)]


def pair_up(axis, first):
    count = lax.axis_size(axis)
    to = list(range(count))
    for i in range(first, count - 1, 2):
        to[i], to[i + 1] = i + 1, i
    return list(enumerate(to))


def moves():
    return ring(ROWS, 1), ring(ROWS, -1), pair_up(TM, 0), pair_up(TM, 1)


def spread_small(x):
    before, after, near, far = moves()
    frames = jnp.concatenate([x, lax.ppermute(x, TM, near), lax.ppermute(x, TM, far)], 0)
    return [frames, lax.ppermute(frames, ROWS, before), lax.ppermute(frames, ROWS, after)]


def then(first, *values):
    return lax.optimization_barrier((first, *values))


ANY = pl.BlockSpec(memory_space=pl.ANY)
VMEM = pl.BlockSpec(memory_space=pltpu.VMEM)
SMEM = pl.BlockSpec(memory_space=pltpu.SMEM)
PARAMS = pltpu.CompilerParams(vmem_limit_bytes=40 * 2**20)


def lists(columns):
    return [pltpu.SMEM((columns * LIST,), jnp.int32), pltpu.SMEM((columns,), jnp.int32)]


def query_call(mask, qg, near_kv, scale):
    columns = mask.shape[0]
    tokens, width = qg.shape[1:]
    tile = tokens // columns
    field = jax.ShapeDtypeStruct((tokens, width), BF16)
    total = pltpu.VMEM((tile, width), F32)
    squares = pltpu.VMEM((27 + GQ - 1, tile, tile), F32)
    return pl.pallas_call(
        lambda *refs: query_kernel(columns, tile, scale, *refs),
        out_shape=(field, field, jax.ShapeDtypeStruct((8, tile), F32)),
        in_specs=[SMEM, ANY] + [ANY] * SLOTS,
        out_specs=(VMEM, VMEM, VMEM),
        scratch_shapes=[
            pltpu.VMEM((SLOTS, 2, tokens, width), BF16),
            pltpu.VMEM((2, tokens, width), BF16),
            squares, squares,
            total, total, total,
            *lists(columns),
            pltpu.SemaphoreType.DMA((SLOTS + 1,)),
        ],
        compiler_params=PARAMS,
        cost_estimate=pl.CostEstimate(
            flops=32 * 5 * 2 * tile * tile * width, bytes_accessed=8 * tokens * width, transcendentals=32 * tile * tile
        ),
        name="query_side",
    )(mask, qg, *near_kv)


def key_call(mask, kv, near_qg, near_stats, scale):
    columns = mask.shape[0]
    tokens, width = kv.shape[1:]
    tile = tokens // columns
    field = jax.ShapeDtypeStruct((tokens, width), BF16)
    total = pltpu.VMEM((tile, width), F32)
    return pl.pallas_call(
        lambda *refs: key_kernel(columns, tile, scale, *refs),
        out_shape=(field, field),
        in_specs=[SMEM, ANY] + [ANY] * SLOTS + [VMEM] * 3,
        out_specs=(VMEM, VMEM),
        scratch_shapes=[
            pltpu.VMEM((SLOTS, 2, tokens, width), BF16),
            pltpu.VMEM((2, tokens, width), BF16),
            pltpu.VMEM((SLOTS + 1, 8, tile), F32),
            total, total,
            *lists(columns),
            pltpu.SemaphoreType.DMA((SLOTS + 1,)),
        ],
        compiler_params=PARAMS,
        cost_estimate=pl.CostEstimate(
            flops=32 * 4 * 2 * tile * tile * width, bytes_accessed=8 * tokens * width, transcendentals=32 * tile * tile
        ),
        name="key_side",
    )(mask, kv, *near_qg, *near_stats)


def body(queries, keys, values, d_out, window_mask):
    columns, tile, width = queries.shape[2], queries.shape[4], queries.shape[5]
    tokens = columns * tile
    scale = width ** -0.5
    flat = lambda x: x.reshape(tokens, width)
    mask = window_mask.reshape(columns, 27)
    pair = jax.ShapeDtypeStruct((2, tokens, width), BF16)
    kv, qg = pl.pallas_call(
        pack_kernel,
        out_shape=(pair, pair),
        in_specs=[VMEM] * 4,
        out_specs=(VMEM, VMEM),
        name="pack",
    )(flat(queries), flat(keys), flat(values), flat(d_out))
    before, after, near, far = moves()
    send = lax.ppermute
    kv_up, kv_down = send(kv, ROWS, before), send(kv, ROWS, after)
    kv_z = send(kv, TM, far)
    kv_o = send(kv, TM, near)
    qg_z = send(qg, TM, far)
    kv_z, kv_up, kv_down, later = then(kv_z, kv_up, kv_down, qg)
    kv_zu, kv_zd = send(kv_z, ROWS, before), send(kv_z, ROWS, after)
    kv_ou, kv_od = send(kv_up, TM, near), send(kv_down, TM, near)
    kv_zu, kv_zd, kv_ou, kv_od, qg_z, later = then(kv_zu, kv_zd, kv_ou, kv_od, qg_z, later)
    qg_up, qg_down = send(later, ROWS, before), send(later, ROWS, after)
    qg_zu, qg_zd = send(qg_z, ROWS, before), send(qg_z, ROWS, after)
    near_kv = [kv, kv_up, kv_down, kv_o, kv_ou, kv_od, kv_z, kv_zu, kv_zd]
    attended, grad_q, stats = query_call(mask, qg, near_kv, scale)
    stats, later, qg_up, qg_down = then(stats, later, qg_up, qg_down)
    near_stats = spread_small(stats)
    qg_o, qg_ou, qg_od = send(later, TM, near), send(qg_up, TM, near), send(qg_down, TM, near)
    near_qg = [qg, qg_up, qg_down, qg_o, qg_ou, qg_od, qg_z, qg_zu, qg_zd]
    grad_k, grad_v = key_call(mask, kv, near_qg, near_stats, scale)
    return tuple(x.reshape(queries.shape) for x in (attended, grad_q, grad_k, grad_v))


def solution(mesh):
    field = P(TM, ROWS, None, "heads", None, None)
    return jax.shard_map(
        body,
        mesh=mesh,
        in_specs=(field, field, field, field, P(TM, ROWS, None, "heads", None)),
        out_specs=(field, field, field, field),
        check_vma=False,
    )
```

```python
import math

import jax
import jax.numpy as jnp
from jax import lax
from jax.experimental import pallas as pl
from jax.experimental.pallas import tpu as pltpu
from jax.sharding import PartitionSpec as P

TM, ROWS = "tm", "rows"
F32, BF16 = jnp.float32, jnp.bfloat16
SLOTS = 9
ROOM = 32
GROUP = 12
LIST = 28
BIG = 6
ROW_STEPS = (0, -1, 1)
NT = (((1,), (1,)), ((), ()))
NN = (((1,), (0,)), ((), ()))


def dot(left, right, dims):
    return lax.dot_general(left, right, dims, preferred_element_type=F32)


def find_pairs(mask, lists, columns):
    near = 1 - 2 * lax.rem(lax.axis_index(TM), 2)
    frame_steps = (0, near, -near)
    n = jnp.int32(0)
    for slot in range(SLOTS):
        dt, dr = frame_steps[slot // 3], ROW_STEPS[slot % 3]
        for c in range(columns):
            for other in range(max(c - 1, 0), min(c + 2, columns)):
                lists[n] = ROOM * c + slot * columns + other
                n = n + mask[0, 0, c, 0, 9 * (dt + 1) + 3 * (dr + 1) + other - c + 1]
    for extra in range(GROUP - 1):
        lists[n + extra] = ROOM * columns
    lists[list_size(columns) - 1] = (n + GROUP - 1) // GROUP


def find_column_pairs(mask, lists, columns):
    near = 1 - 2 * lax.rem(lax.axis_index(TM), 2)
    frame_steps = (0, near, -near)
    for c in range(columns):
        n = jnp.int32(0)
        for slot in range(SLOTS):
            dt, dr = frame_steps[slot // 3], ROW_STEPS[slot % 3]
            for other in range(max(c - 1, 0), min(c + 2, columns)):
                lists[c * LIST + n] = slot * columns + other
                n = n + mask[0, 0, c, 0, 9 * (dt + 1) + 3 * (dr + 1) + other - c + 1]
        lists[c * LIST + n] = c
        lists[columns * LIST + c] = n


def list_size(columns):
    return 27 * columns + GROUP


def pack_kernel(columns, mask, q, k, v, g, kv, qg, pairs, column_pairs):
    kv[0], kv[1], qg[0], qg[1] = k[...], v[...], q[...], g[...]
    find_pairs(mask, pairs, columns)
    find_column_pairs(mask, column_pairs, columns)


def fetch(own, slots, near, mine, sems):
    tokens = own[0].shape[0]
    copies = []
    for i in range(4):
        to = near if i < 2 else mine
        copies.append(pltpu.make_async_copy(own[i], to.at[i % 2, pl.ds(0, tokens)], sems.at[i]))
    for s in range(1, SLOTS):
        at = pl.ds(s * tokens, tokens)
        halves = len(slots) - SLOTS + 1
        if s <= len(slots) - 2 * halves:
            copies.append(pltpu.make_async_copy(slots[s - 1], near.at[:, at], sems.at[s + 3]))
        else:
            for i in range(2):
                n = 2 * s + i - SLOTS + halves - 1
                copies.append(pltpu.make_async_copy(slots[n], near.at[i, at], sems.at[n + 4]))
    for copy in copies:
        copy.start()
    return copies


def for_groups(columns, lists, run):
    def step(i, carry):
        at = [GROUP * i + j for j in range(GROUP)]
        entries = [lists[place] for place in at]
        run(at, [entry // ROOM for entry in entries], [lax.rem(entry, ROOM) for entry in entries])
        return carry

    lax.fori_loop(0, lists[list_size(columns) - 1], step, 0)


def query_kernel(columns, tile, scale, lists, *refs):
    own, slots = refs[:4], refs[4:SLOTS + 6]
    out, grad_q, stats = refs[SLOTS + 6:SLOTS + 9]
    near, mine, s_all, w_all, top, low, acc, sems = refs[SLOTS + 9:]
    copies = fetch(own, slots, near, mine, sems)
    unit = scale * math.log2(math.e)
    top[...] = jnp.full(top.shape, -jnp.inf, F32)
    low[...] = jnp.zeros(low.shape, F32)
    acc[...] = jnp.zeros(acc.shape, F32)
    for copy in copies:
        copy.wait()

    def rows(index):
        return pl.ds(pl.multiple_of(index * tile, tile), tile)

    def wide(x):
        return jnp.concatenate([x, x], 1)

    def score_step(at, ours, tiles):
        for place, c, t in zip(at, ours, tiles):
            s = dot(mine[0, rows(c), :], near[0, rows(t), :], NT) * unit
            s_all[place] = s
            top[rows(c), :] = jnp.maximum(top[rows(c), :], jnp.maximum(s[:, :128], s[:, 128:]))

    for_groups(columns, lists, score_step)
    for c in range(columns):
        own_rows = slice(c * tile, (c + 1) * tile)
        peak = jnp.max(top[own_rows, :], axis=1, keepdims=True)
        top[own_rows, :] = jnp.broadcast_to(peak, (tile, 128))

    def value_step(at, ours, tiles):
        for place, c, t in zip(at, ours, tiles):
            v = near[1, rows(t), :]
            e = jnp.exp2(s_all[place] - wide(top[rows(c), :]))
            s_all[place] = e
            w_all[place] = dot(mine[1, rows(c), :], v, NT)
            low[rows(c), :] += e[:, :128] + e[:, 128:]
            acc[rows(c), :] += dot(e.astype(BF16), v, NN)

    for_groups(columns, lists, value_step)
    lane = lax.broadcasted_iota(jnp.int32, (tile, 128), 1)
    for c in range(columns):
        own_rows = slice(c * tile, (c + 1) * tile)
        total = jnp.sum(low[own_rows, :], axis=1, keepdims=True)
        inverse = 1.0 / total
        attended = (acc[own_rows, :] * inverse).astype(BF16)
        out[own_rows, :] = attended
        delta = jnp.sum(mine[1, own_rows, :].astype(F32) * attended.astype(F32), axis=1, keepdims=True)
        both = jnp.where(lane == 0, top[own_rows, :] + jnp.log2(total), delta).T
        stats[c:c + 1, :] = both[0:1]
        stats[4 + c:5 + c, :] = both[1:2]
        top[own_rows, :] = jnp.broadcast_to(delta, (tile, 128))
        low[own_rows, :] = jnp.broadcast_to(inverse * scale, (tile, 128))
        acc[own_rows, :] = jnp.zeros((tile, 128), F32)

    def query_step(at, ours, tiles):
        for place, c, t in zip(at, ours, tiles):
            ds = s_all[place] * (w_all[place] - wide(top[rows(c), :]))
            acc[rows(c), :] += dot(ds.astype(BF16), near[0, rows(t), :], NN)

    for_groups(columns, lists, query_step)
    grad_q[...] = (acc[:columns * tile, :] * low[:columns * tile, :]).astype(BF16)


def grouped(n, run):
    many = n // BIG

    def big(i, carry):
        run(BIG * i, BIG)
        return carry

    def small(i, carry):
        run(BIG * many + 2 * i, 2)
        return carry

    lax.fori_loop(0, many, big, 0)
    lax.fori_loop(0, (n - BIG * many + 1) // 2, small, 0)


def key_kernel(columns, tile, scale, lists, *refs):
    own, slots, sets = refs[:4], refs[4:SLOTS + 6], refs[SLOTS + 6:SLOTS + 9]
    grad_k, grad_v, near, mine, logs, deltas, k_acc, v_acc, sems = refs[SLOTS + 9:]
    copies = fetch(own, slots, near, mine, sems)
    for slot in range(SLOTS):
        first = 8 * (slot // 3)
        logs[slot * columns:(slot + 1) * columns, :] = sets[slot % 3][first:first + columns, :]
        deltas[slot * columns:(slot + 1) * columns, :] = sets[slot % 3][first + 4:first + 4 + columns, :]
    logs[SLOTS * columns:, :] = jnp.full((5, tile), 1e30, F32)
    for copy in copies:
        copy.wait()
    unit = scale * math.log2(math.e)

    def one_column(c, carry):
        rows = pl.ds(pl.multiple_of(c * tile, tile), tile)
        n = lists[columns * LIST + c]
        k_acc[...] = jnp.zeros(k_acc.shape, F32)
        v_acc[...] = jnp.zeros(v_acc.shape, F32)

        def step(first, size):
            k = mine[0, rows, :]
            v = mine[1, rows, :]
            sum_v = v_acc[...]
            sum_k = k_acc[...]
            for j in range(size):
                t = lists[c * LIST + first + j]
                at = pl.ds(pl.multiple_of(t * tile, tile), tile)
                q, g = near[0, at, :], near[1, at, :]
                held = jnp.where(first + j < n, t, SLOTS * columns) if size == 2 and j == 1 else t
                log_total = logs[pl.ds(held, 1), :]
                delta = deltas[pl.ds(t, 1), :]
                p = jnp.exp2(dot(k, q, NT) * unit - log_total)
                sum_v = sum_v + dot(p.astype(BF16), g, NN)
                ds = p * (dot(v, g, NT) - delta)
                sum_k = sum_k + dot(ds.astype(BF16), q, NN)
            v_acc[...] = sum_v
            k_acc[...] = sum_k

        grouped(n, step)
        grad_k[rows, :] = (k_acc[...] * scale).astype(BF16)
        grad_v[rows, :] = v_acc[...].astype(BF16)
        return carry

    lax.fori_loop(0, columns, one_column, 0)


def ring(axis, step):
    count = lax.axis_size(axis)
    return [(i, (i + step) % count) for i in range(count)]


def pair_up(axis, first):
    count = lax.axis_size(axis)
    to = list(range(count))
    for i in range(first, count - 1, 2):
        to[i], to[i + 1] = i + 1, i
    return list(enumerate(to))


def moves():
    return ring(ROWS, 1), ring(ROWS, -1), pair_up(TM, 0), pair_up(TM, 1)


def spread_small(x):
    before, after, near, far = moves()
    frames = jnp.concatenate([x, lax.ppermute(x, TM, near), lax.ppermute(x, TM, far)], 0)
    return [frames, lax.ppermute(frames, ROWS, before), lax.ppermute(frames, ROWS, after)]


def then(first, *values):
    return lax.optimization_barrier((first, *values))


ANY = pl.BlockSpec(memory_space=pl.ANY)
VMEM = pl.BlockSpec(memory_space=pltpu.VMEM)
HBM = pl.BlockSpec(memory_space=pltpu.HBM)
SMEM = pl.BlockSpec(memory_space=pltpu.SMEM)
PARAMS = pltpu.CompilerParams(vmem_limit_bytes=52 * 2**20)


def query_call(columns, lists, q, k, v, g, near_kv, scale):
    tokens, width = q.shape
    tile = tokens // columns
    field = jax.ShapeDtypeStruct((tokens, width), BF16)
    total = pltpu.VMEM(((columns + 1) * tile, width), F32)
    squares = pltpu.VMEM((list_size(columns) - 18, tile, tile), F32)
    return pl.pallas_call(
        lambda *refs: query_kernel(columns, tile, scale, *refs),
        out_shape=(field, field, jax.ShapeDtypeStruct((8, tile), F32)),
        in_specs=[SMEM] + [HBM] * 4 + [ANY] * (SLOTS + 2),
        out_specs=(VMEM, VMEM, VMEM),
        scratch_shapes=[
            pltpu.VMEM((2, SLOTS * tokens, width), BF16),
            pltpu.VMEM((2, tokens + tile, width), BF16),
            squares, squares,
            total, total, total,
            pltpu.SemaphoreType.DMA((SLOTS + 6,)),
        ],
        compiler_params=PARAMS,
        cost_estimate=pl.CostEstimate(
            flops=32 * 5 * 2 * tile * tile * width, bytes_accessed=8 * tokens * width, transcendentals=32 * tile * tile
        ),
        name="query_side",
    )(lists, k, v, q, g, *near_kv)


def key_call(columns, lists, q, k, v, g, near_qg, near_stats, scale):
    tokens, width = q.shape
    tile = tokens // columns
    field = jax.ShapeDtypeStruct((tokens, width), BF16)
    total = pltpu.VMEM((tile, width), F32)
    return pl.pallas_call(
        lambda *refs: key_kernel(columns, tile, scale, *refs),
        out_shape=(field, field),
        in_specs=[SMEM] + [HBM] * 4 + [ANY] * (SLOTS + 2) + [VMEM] * 3,
        out_specs=(VMEM, VMEM),
        scratch_shapes=[
            pltpu.VMEM((2, SLOTS * tokens, width), BF16),
            pltpu.VMEM((2, tokens + tile, width), BF16),
            *[pltpu.VMEM((SLOTS * columns + 5, tile), F32)] * 2,
            total, total,
            pltpu.SemaphoreType.DMA((SLOTS + 6,)),
        ],
        compiler_params=PARAMS,
        cost_estimate=pl.CostEstimate(
            flops=32 * 4 * 2 * tile * tile * width, bytes_accessed=8 * tokens * width, transcendentals=32 * tile * tile
        ),
        name="key_side",
    )(lists, q, g, k, v, *near_qg, *near_stats)


def body(queries, keys, values, d_out, window_mask):
    columns, tile, width = queries.shape[2], queries.shape[4], queries.shape[5]
    tokens = columns * tile
    scale = width ** -0.5
    flat = lambda x: x.reshape(tokens, width)
    pair = jax.ShapeDtypeStruct((2, tokens, width), BF16)
    own = [flat(x) for x in (queries, keys, values, d_out)]
    kv, qg, pairs, column_pairs = pl.pallas_call(
        lambda *refs: pack_kernel(columns, *refs),
        out_shape=(
            pair, pair,
            jax.ShapeDtypeStruct((list_size(columns),), jnp.int32),
            jax.ShapeDtypeStruct((columns * (LIST + 1),), jnp.int32),
        ),
        in_specs=[SMEM] + [VMEM] * 4,
        out_specs=(VMEM, VMEM, SMEM, SMEM),
        name="pack",
    )(window_mask, *own)
    before, after, near, far = moves()
    send = lax.ppermute
    kv_o = send(kv, TM, near)
    kv_up, kv_down = send(kv, ROWS, before), send(kv, ROWS, after)
    frame = lax.axis_index(TM)
    inner = (frame > 0) & (frame < lax.axis_size(TM) - 1)
    half = send(jnp.where(inner, kv[0], kv_o[1]), TM, ring(TM, 2))
    qg_o = send(qg, TM, near)
    qg_half = send(jnp.where(inner, qg[0], qg_o[1]), TM, ring(TM, 2))
    half, qg_next = then(half, qg)
    half_up, half_down = send(half, ROWS, before), send(half, ROWS, after)
    rest = send(half, TM, near)
    kv_ou, kv_od = send(kv_up, TM, near), send(kv_down, TM, near)
    qg_up, qg_down = send(qg_next, ROWS, before), send(qg_next, ROWS, after)
    qg_half, half_up, half_down = then(qg_half, half_up, half_down)
    rest_up, rest_down = send(half_up, TM, near), send(half_down, TM, near)
    qg_half_up, qg_half_down = send(qg_half, ROWS, before), send(qg_half, ROWS, after)
    near_kv = [kv_up, kv_down, kv_o, kv_ou, kv_od, rest, half, rest_up, half_up, rest_down, half_down]
    attended, grad_q, stats = query_call(columns, pairs, *own, near_kv, scale)
    stats, qg_half, qg_up, qg_down, qg_half_up, qg_half_down = then(
        stats, qg_half, qg_up, qg_down, qg_half_up, qg_half_down
    )
    near_stats = spread_small(stats)
    qg_ou, qg_od = send(qg_up, TM, near), send(qg_down, TM, near)
    qg_rest, qg_rest_up, qg_rest_down = [send(x, TM, near) for x in (qg_half, qg_half_up, qg_half_down)]
    near_qg = [
        qg_up, qg_down, qg_o, qg_ou, qg_od, qg_rest, qg_half, qg_rest_up, qg_half_up, qg_rest_down, qg_half_down
    ]
    grad_k, grad_v = key_call(columns, column_pairs, *own, near_qg, near_stats, scale)
    return tuple(x.reshape(queries.shape) for x in (attended, grad_q, grad_k, grad_v))


def solution(mesh):
    field = P(TM, ROWS, None, "heads", None, None)
    return jax.shard_map(
        body,
        mesh=mesh,
        in_specs=(field, field, field, field, P(TM, ROWS, None, "heads", None)),
        out_specs=(field, field, field, field),
        check_vma=False,
    )
```

```python
import math

import jax
import jax.numpy as jnp
from jax import lax
from jax.experimental import pallas as pl
from jax.experimental.pallas import tpu as pltpu
from jax.sharding import PartitionSpec as P

TM, ROWS = "tm", "rows"
F32, BF16 = jnp.float32, jnp.bfloat16
SLOTS = 9
ROOM = 32
GROUP = 12
SUB = 3
TURN = 3
ROW_STEPS = (0, -1, 1)
NT = (((1,), (1,)), ((), ()))
NN = (((1,), (0,)), ((), ()))


def dot(left, right, dims):
    return lax.dot_general(left, right, dims, preferred_element_type=F32)


def find_pairs(mask, lists, columns):
    near = 1 - 2 * lax.rem(lax.axis_index(TM), 2)
    frame_steps = (0, near, -near)
    n = jnp.int32(0)
    for slot in range(SLOTS):
        dt, dr = frame_steps[slot // 3], ROW_STEPS[slot % 3]
        for c in range(columns):
            for other in range(max(c - 1, 0), min(c + 2, columns)):
                lists[n] = ROOM * c + slot * columns + other
                n = n + mask[0, 0, c, 0, 9 * (dt + 1) + 3 * (dr + 1) + other - c + 1]
    for extra in range(GROUP - 1):
        lists[n + extra] = ROOM * columns
    lists[list_size(columns) - 1] = (n + GROUP - 1) // GROUP


def list_size(columns):
    return 27 * columns + GROUP


def find_subgroups(mask, lists, columns):
    near = 1 - 2 * lax.rem(lax.axis_index(TM), 2)
    frame_steps = (0, near, -near)
    n = jnp.int32(0)
    for c in range(columns):
        for slot in range(SLOTS):
            dt, dr = frame_steps[slot // 3], ROW_STEPS[slot % 3]
            for other in range(max(c - 1, 0), min(c + 2, columns)):
                lists[n] = slot * columns + other
                n = n + mask[0, 0, c, 0, 9 * (dt + 1) + 3 * (dr + 1) + other - c + 1]
        for extra in range(SUB - 1):
            lists[n + extra] = SLOTS * columns
        end = (n + SUB - 1) // SUB
        lists[places(columns) - columns + c] = end
        n = end * SUB
    for extra in range(SUB * (TURN - 1)):
        lists[n + extra] = SLOTS * columns


def subgroups(columns):
    most = sum(-(-9 * (min(c + 2, columns) - max(c - 1, 0)) // SUB) for c in range(columns))
    return -(-most // TURN) * TURN


def places(columns):
    return (subgroups(columns) + TURN) * SUB + columns


def pack_kv_kernel(k, v, kv):
    kv[0], kv[1] = k[...], v[...]


def pack_qg_kernel(columns, mask, q, g, qg, pairs, subgroup_pairs):
    qg[0], qg[1] = q[...], g[...]
    find_pairs(mask, pairs, columns)
    find_subgroups(mask, subgroup_pairs, columns)


def fetch(own, slots, near, mine, sems):
    tokens = own[0].shape[0]
    copies = []
    for i in range(4):
        to = near if i < 2 else mine
        copies.append(pltpu.make_async_copy(own[i], to.at[i % 2, pl.ds(0, tokens)], sems.at[i]))
    for s in range(1, SLOTS):
        at = pl.ds(s * tokens, tokens)
        halves = len(slots) - SLOTS + 1
        if s <= len(slots) - 2 * halves:
            copies.append(pltpu.make_async_copy(slots[s - 1], near.at[:, at], sems.at[s + 3]))
        else:
            for i in range(2):
                n = 2 * s + i - SLOTS + halves - 1
                copies.append(pltpu.make_async_copy(slots[n], near.at[i, at], sems.at[n + 4]))
    for copy in copies:
        copy.start()
    return copies


def for_groups(columns, lists, run):
    def step(i, carry):
        at = [GROUP * i + j for j in range(GROUP)]
        entries = [lists[place] for place in at]
        run(at, [entry // ROOM for entry in entries], [lax.rem(entry, ROOM) for entry in entries])
        return carry

    lax.fori_loop(0, lists[list_size(columns) - 1], step, 0)


def query_kernel(columns, tile, scale, lists, *refs):
    own, slots = refs[:4], refs[4:SLOTS + 6]
    out, grad_q, stats = refs[SLOTS + 6:SLOTS + 9]
    near, mine, s_all, w_all, top, low, acc, sems = refs[SLOTS + 9:]
    copies = fetch(own, slots, near, mine, sems)
    unit = scale * math.log2(math.e)
    top[...] = jnp.full(top.shape, -jnp.inf, F32)
    low[...] = jnp.zeros(low.shape, F32)
    acc[...] = jnp.zeros(acc.shape, F32)
    for copy in copies:
        copy.wait()

    def rows(index):
        return pl.ds(pl.multiple_of(index * tile, tile), tile)

    def wide(x):
        return jnp.concatenate([x, x], 1)

    def score_step(at, ours, tiles):
        for place, c, t in zip(at, ours, tiles):
            s = dot(mine[0, rows(c), :], near[0, rows(t), :], NT) * unit
            s_all[place] = s
            top[rows(c), :] = jnp.maximum(top[rows(c), :], jnp.maximum(s[:, :128], s[:, 128:]))

    for_groups(columns, lists, score_step)
    for c in range(columns):
        own_rows = slice(c * tile, (c + 1) * tile)
        peak = jnp.max(top[own_rows, :], axis=1, keepdims=True)
        top[own_rows, :] = jnp.broadcast_to(peak, (tile, 128))

    def value_step(at, ours, tiles):
        for place, c, t in zip(at, ours, tiles):
            v = near[1, rows(t), :]
            e = jnp.exp2(s_all[place] - wide(top[rows(c), :]))
            s_all[place] = e
            w_all[place] = dot(mine[1, rows(c), :], v, NT)
            low[rows(c), :] += e[:, :128] + e[:, 128:]
            acc[rows(c), :] += dot(e.astype(BF16), v, NN)

    for_groups(columns, lists, value_step)
    lane = lax.broadcasted_iota(jnp.int32, (tile, 128), 1)
    for c in range(columns):
        own_rows = slice(c * tile, (c + 1) * tile)
        total = jnp.sum(low[own_rows, :], axis=1, keepdims=True)
        inverse = 1.0 / total
        attended = (acc[own_rows, :] * inverse).astype(BF16)
        out[own_rows, :] = attended
        delta = jnp.sum(mine[1, own_rows, :].astype(F32) * attended.astype(F32), axis=1, keepdims=True)
        both = jnp.where(lane == 0, top[own_rows, :] + jnp.log2(total), delta).T
        stats[c:c + 1, :] = both[0:1]
        stats[4 + c:5 + c, :] = both[1:2]
        top[own_rows, :] = jnp.broadcast_to(delta, (tile, 128))
        low[own_rows, :] = jnp.broadcast_to(inverse * scale, (tile, 128))
        acc[own_rows, :] = jnp.zeros((tile, 128), F32)

    def query_step(at, ours, tiles):
        for place, c, t in zip(at, ours, tiles):
            ds = s_all[place] * (w_all[place] - wide(top[rows(c), :]))
            acc[rows(c), :] += dot(ds.astype(BF16), near[0, rows(t), :], NN)

    for_groups(columns, lists, query_step)
    grad_q[...] = (acc[:columns * tile, :] * low[:columns * tile, :]).astype(BF16)


def for_turns(columns, lists, run):
    ends = [lists[places(columns) - columns + c] for c in range(columns)]

    def step(i, carry):
        subs = []
        for j in range(TURN):
            at = TURN * i + j
            column = sum([(at >= end).astype(jnp.int32) for end in ends[:-1]], jnp.int32(0))
            subs.append((column, [lists[SUB * at + p] for p in range(SUB)]))
        run(i, subs)
        return carry

    lax.fori_loop(0, (ends[-1] + TURN - 1) // TURN, step, 0)


def key_kernel(columns, tile, scale, lists, *refs):
    own, slots, sets = refs[:4], refs[4:SLOTS + 6], refs[SLOTS + 6:SLOTS + 9]
    grad_k, grad_v, near, mine, logs, deltas, k_acc, v_acc, sems = refs[SLOTS + 9:SLOTS + 18]
    probs, scores = refs[SLOTS + 18:SLOTS + 18 + TURN], refs[SLOTS + 18 + TURN:]
    copies = fetch(own, slots, near, mine, sems)
    spare = pl.ds(SLOTS * columns * tile, tile)
    near[:, spare] = jnp.zeros((2, tile, near.shape[2]), BF16)
    for slot in range(SLOTS):
        first = 8 * (slot // 3)
        logs[slot * columns:(slot + 1) * columns, :] = sets[slot % 3][first:first + columns, :]
        deltas[slot * columns:(slot + 1) * columns, :] = sets[slot % 3][first + 4:first + 4 + columns, :]
    logs[SLOTS * columns:, :] = jnp.full((5, tile), 1e30, F32)
    deltas[SLOTS * columns:, :] = jnp.zeros((5, tile), F32)
    k_acc[...] = jnp.zeros(k_acc.shape, F32)
    v_acc[...] = jnp.zeros(v_acc.shape, F32)
    for copy in copies:
        copy.wait()
    unit = scale * math.log2(math.e)

    def rows(index):
        return pl.ds(pl.multiple_of(index * tile, tile), tile)

    def stacked(which, tiles):
        return jnp.concatenate([near[which, rows(t), :] for t in tiles], 0)

    def step(i, subs):
        for j, (c, tiles) in enumerate(subs):
            k, v = mine[0, rows(c), :], mine[1, rows(c), :]
            for n, t in enumerate(tiles):
                part = slice(n * tile, (n + 1) * tile)
                p = jnp.exp2(dot(k, near[0, rows(t), :], NT) * unit - logs[pl.ds(t, 1), :])
                probs[j][:, part] = p.astype(BF16)
                w = dot(v, near[1, rows(t), :], NT) - deltas[pl.ds(t, 1), :]
                scores[j][:, part] = (p * w).astype(BF16)
            v_acc[rows(c), :] += dot(probs[j][...], stacked(1, tiles), NN)
            k_acc[rows(c), :] += dot(scores[j][...], stacked(0, tiles), NN)

    for_turns(columns, lists, step)
    grad_k[...] = (k_acc[...] * scale).astype(BF16)
    grad_v[...] = v_acc[...].astype(BF16)


def ring(axis, step):
    count = lax.axis_size(axis)
    return [(i, (i + step) % count) for i in range(count)]


def pair_up(axis, first):
    count = lax.axis_size(axis)
    to = list(range(count))
    for i in range(first, count - 1, 2):
        to[i], to[i + 1] = i + 1, i
    return list(enumerate(to))


def moves():
    return ring(ROWS, 1), ring(ROWS, -1), pair_up(TM, 0), pair_up(TM, 1)


def spread_small(x):
    before, after, near, far = moves()
    frames = jnp.concatenate([x, lax.ppermute(x, TM, near), lax.ppermute(x, TM, far)], 0)
    return [frames, lax.ppermute(frames, ROWS, before), lax.ppermute(frames, ROWS, after)]


def then(first, *values):
    return lax.optimization_barrier((first, *values))


ANY = pl.BlockSpec(memory_space=pl.ANY)
VMEM = pl.BlockSpec(memory_space=pltpu.VMEM)
HBM = pl.BlockSpec(memory_space=pltpu.HBM)
SMEM = pl.BlockSpec(memory_space=pltpu.SMEM)
PARAMS = pltpu.CompilerParams(vmem_limit_bytes=52 * 2**20)


def query_call(columns, lists, q, k, v, g, near_kv, scale):
    tokens, width = q.shape
    tile = tokens // columns
    field = jax.ShapeDtypeStruct((tokens, width), BF16)
    total = pltpu.VMEM(((columns + 1) * tile, width), F32)
    squares = pltpu.VMEM((list_size(columns) - 18, tile, tile), F32)
    return pl.pallas_call(
        lambda *refs: query_kernel(columns, tile, scale, *refs),
        out_shape=(field, field, jax.ShapeDtypeStruct((8, tile), F32)),
        in_specs=[SMEM] + [HBM] * 4 + [ANY] * (SLOTS + 2),
        out_specs=(VMEM, VMEM, VMEM),
        scratch_shapes=[
            pltpu.VMEM((2, SLOTS * tokens, width), BF16),
            pltpu.VMEM((2, tokens + tile, width), BF16),
            squares, squares,
            total, total, total,
            pltpu.SemaphoreType.DMA((SLOTS + 6,)),
        ],
        compiler_params=PARAMS,
        cost_estimate=pl.CostEstimate(
            flops=32 * 5 * 2 * tile * tile * width, bytes_accessed=8 * tokens * width, transcendentals=32 * tile * tile
        ),
        name="query_side",
    )(lists, k, v, q, g, *near_kv)


def key_call(columns, lists, q, k, v, g, near_qg, near_stats, scale):
    tokens, width = q.shape
    tile = tokens // columns
    field = jax.ShapeDtypeStruct((tokens, width), BF16)
    total = pltpu.VMEM((tokens, width), F32)
    return pl.pallas_call(
        lambda *refs: key_kernel(columns, tile, scale, *refs),
        out_shape=(field, field),
        in_specs=[SMEM] + [HBM] * 4 + [ANY] * (SLOTS + 2) + [VMEM] * 3,
        out_specs=(VMEM, VMEM),
        scratch_shapes=[
            pltpu.VMEM((2, SLOTS * tokens + tile, width), BF16),
            pltpu.VMEM((2, tokens, width), BF16),
            *[pltpu.VMEM((SLOTS * columns + 5, tile), F32)] * 2,
            total, total,
            pltpu.SemaphoreType.DMA((SLOTS + 6,)),
            *[pltpu.VMEM((tile, SUB * tile), BF16)] * (2 * TURN),
        ],
        compiler_params=PARAMS,
        cost_estimate=pl.CostEstimate(
            flops=32 * 4 * 2 * tile * tile * width, bytes_accessed=8 * tokens * width, transcendentals=32 * tile * tile
        ),
        name="key_side",
    )(lists, q, g, k, v, *near_qg, *near_stats)


def body(queries, keys, values, d_out, window_mask):
    columns, tile, width = queries.shape[2], queries.shape[4], queries.shape[5]
    tokens = columns * tile
    scale = width ** -0.5
    flat = lambda x: x.reshape(tokens, width)
    pair = jax.ShapeDtypeStruct((2, tokens, width), BF16)
    own = [flat(x) for x in (queries, keys, values, d_out)]
    q, k, v, g = own
    kv = pl.pallas_call(pack_kv_kernel, out_shape=pair, in_specs=[VMEM] * 2, out_specs=VMEM, name="pack_kv")(k, v)
    before, after, near, far = moves()
    send = lax.ppermute
    kv_o = send(kv, TM, near)
    kv_up, kv_down = send(kv, ROWS, before), send(kv, ROWS, after)
    kv_o, q, g = then(kv_o, q, g)
    qg, pairs, subgroup_pairs = pl.pallas_call(
        lambda *refs: pack_qg_kernel(columns, *refs),
        out_shape=(
            pair,
            jax.ShapeDtypeStruct((list_size(columns),), jnp.int32),
            jax.ShapeDtypeStruct((places(columns),), jnp.int32),
        ),
        in_specs=[SMEM] + [VMEM] * 2,
        out_specs=(VMEM, SMEM, SMEM),
        name="pack_qg",
    )(window_mask, q, g)
    frame = lax.axis_index(TM)
    inner = (frame > 0) & (frame < lax.axis_size(TM) - 1)
    half = send(jnp.where(inner, kv[0], kv_o[1]), TM, ring(TM, 2))
    qg_o = send(qg, TM, near)
    qg_half = send(jnp.where(inner, qg[0], qg_o[1]), TM, ring(TM, 2))
    half, qg_next = then(half, qg)
    half_up, half_down = send(half, ROWS, before), send(half, ROWS, after)
    rest = send(half, TM, near)
    kv_ou, kv_od = send(kv_up, TM, near), send(kv_down, TM, near)
    qg_up, qg_down = send(qg_next, ROWS, before), send(qg_next, ROWS, after)
    qg_half, half_up, half_down = then(qg_half, half_up, half_down)
    rest_up, rest_down = send(half_up, TM, near), send(half_down, TM, near)
    qg_half_up, qg_half_down = send(qg_half, ROWS, before), send(qg_half, ROWS, after)
    near_kv = [kv_up, kv_down, kv_o, kv_ou, kv_od, rest, half, rest_up, half_up, rest_down, half_down]
    attended, grad_q, stats = query_call(columns, pairs, *own, near_kv, scale)
    stats, qg_half, qg_up, qg_down, qg_half_up, qg_half_down = then(
        stats, qg_half, qg_up, qg_down, qg_half_up, qg_half_down
    )
    near_stats = spread_small(stats)
    qg_ou, qg_od = send(qg_up, TM, near), send(qg_down, TM, near)
    qg_rest, qg_rest_up, qg_rest_down = [send(x, TM, near) for x in (qg_half, qg_half_up, qg_half_down)]
    near_qg = [
        qg_up, qg_down, qg_o, qg_ou, qg_od, qg_rest, qg_half, qg_rest_up, qg_half_up, qg_rest_down, qg_half_down
    ]
    grad_k, grad_v = key_call(columns, subgroup_pairs, *own, near_qg, near_stats, scale)
    return tuple(x.reshape(queries.shape) for x in (attended, grad_q, grad_k, grad_v))


def solution(mesh):
    field = P(TM, ROWS, None, "heads", None, None)
    return jax.shard_map(
        body,
        mesh=mesh,
        in_specs=(field, field, field, field, P(TM, ROWS, None, "heads", None)),
        out_specs=(field, field, field, field),
        check_vma=False,
    )
```

```python
import math

import jax
import jax.numpy as jnp
from jax import lax
from jax.experimental import pallas as pl
from jax.experimental.pallas import tpu as pltpu
from jax.sharding import PartitionSpec as P

TM, ROWS = "tm", "rows"
F32, BF16 = jnp.float32, jnp.bfloat16
SLOTS = 9
ROOM = 32
GROUP = 14
SUB = 3
TURN = 3
ROW_STEPS = (0, -1, 1)
NT = (((1,), (1,)), ((), ()))
NN = (((1,), (0,)), ((), ()))


def dot(left, right, dims):
    return lax.dot_general(left, right, dims, preferred_element_type=F32)


def find_pairs(mask, lists, columns):
    near = 1 - 2 * lax.rem(lax.axis_index(TM), 2)
    frame_steps = (0, near, -near)
    n = jnp.int32(0)
    for slot in range(SLOTS):
        dt, dr = frame_steps[slot // 3], ROW_STEPS[slot % 3]
        for c in range(columns):
            for other in range(max(c - 1, 0), min(c + 2, columns)):
                lists[n] = ROOM * c + slot * columns + other
                n = n + mask[0, 0, c, 0, 9 * (dt + 1) + 3 * (dr + 1) + other - c + 1]
    for extra in range(GROUP - 1):
        lists[n + extra] = ROOM * columns
    lists[list_size(columns) - 1] = (n + GROUP - 1) // GROUP


def list_size(columns):
    return 27 * columns + GROUP


def find_subgroups(mask, lists, columns):
    near = 1 - 2 * lax.rem(lax.axis_index(TM), 2)
    frame_steps = (0, near, -near)
    n = jnp.int32(0)
    for c in range(columns):
        for slot in range(SLOTS):
            dt, dr = frame_steps[slot // 3], ROW_STEPS[slot % 3]
            for other in range(max(c - 1, 0), min(c + 2, columns)):
                lists[n] = slot * columns + other
                n = n + mask[0, 0, c, 0, 9 * (dt + 1) + 3 * (dr + 1) + other - c + 1]
        for extra in range(SUB - 1):
            lists[n + extra] = SLOTS * columns
        end = (n + SUB - 1) // SUB
        lists[places(columns) - columns + c] = end
        n = end * SUB
    for extra in range(SUB * (TURN - 1)):
        lists[n + extra] = SLOTS * columns


def subgroups(columns):
    most = sum(-(-9 * (min(c + 2, columns) - max(c - 1, 0)) // SUB) for c in range(columns))
    return -(-most // TURN) * TURN


def places(columns):
    return (subgroups(columns) + TURN) * SUB + columns


def pack_kernel(columns, mask, q, k, v, g, kv, qg, pairs, subgroup_pairs):
    kv[0], kv[1], qg[0], qg[1] = k[...], v[...], q[...], g[...]
    find_pairs(mask, pairs, columns)
    find_subgroups(mask, subgroup_pairs, columns)


def fetch(own, slots, near, mine, sems):
    tokens = own[0].shape[0]
    copies = []
    for i in range(4):
        to = near if i < 2 else mine
        copies.append(pltpu.make_async_copy(own[i], to.at[i % 2, pl.ds(0, tokens)], sems.at[i]))
    for s in range(1, SLOTS):
        at = pl.ds(s * tokens, tokens)
        halves = len(slots) - SLOTS + 1
        if s <= len(slots) - 2 * halves:
            copies.append(pltpu.make_async_copy(slots[s - 1], near.at[:, at], sems.at[s + 3]))
        else:
            for i in range(2):
                n = 2 * s + i - SLOTS + halves - 1
                copies.append(pltpu.make_async_copy(slots[n], near.at[i, at], sems.at[n + 4]))
    for copy in copies:
        copy.start()
    return copies


def for_groups(columns, lists, run):
    def step(i, carry):
        at = [GROUP * i + j for j in range(GROUP)]
        entries = [lists[place] for place in at]
        run(at, [entry // ROOM for entry in entries], [lax.rem(entry, ROOM) for entry in entries])
        return carry

    lax.fori_loop(0, lists[list_size(columns) - 1], step, 0)


def query_kernel(columns, tile, scale, lists, *refs):
    own, slots = refs[:4], refs[4:SLOTS + 6]
    out, grad_q, stats = refs[SLOTS + 6:SLOTS + 9]
    near, mine, s_all, w_all, top, low, acc, sems = refs[SLOTS + 9:]
    copies = fetch(own, slots, near, mine, sems)
    unit = scale * math.log2(math.e)
    top[...] = jnp.full(top.shape, -jnp.inf, F32)
    low[...] = jnp.zeros(low.shape, F32)
    acc[...] = jnp.zeros(acc.shape, F32)
    for copy in copies:
        copy.wait()

    def rows(index):
        return pl.ds(pl.multiple_of(index * tile, tile), tile)

    def wide(x):
        return jnp.concatenate([x, x], 1)

    def score_step(at, ours, tiles):
        for place, c, t in zip(at, ours, tiles):
            s = dot(mine[0, rows(c), :], near[0, rows(t), :], NT) * unit
            s_all[place] = s
            top[rows(c), :] = jnp.maximum(top[rows(c), :], jnp.maximum(s[:, :128], s[:, 128:]))

    for_groups(columns, lists, score_step)
    for c in range(columns):
        own_rows = slice(c * tile, (c + 1) * tile)
        peak = jnp.max(top[own_rows, :], axis=1, keepdims=True)
        top[own_rows, :] = jnp.broadcast_to(peak, (tile, 128))

    def value_step(at, ours, tiles):
        for place, c, t in zip(at, ours, tiles):
            v = near[1, rows(t), :]
            e = jnp.exp2(s_all[place] - wide(top[rows(c), :]))
            s_all[place] = e
            w_all[place] = dot(mine[1, rows(c), :], v, NT)
            low[rows(c), :] += e[:, :128] + e[:, 128:]
            acc[rows(c), :] += dot(e.astype(BF16), v, NN)

    for_groups(columns, lists, value_step)
    lane = lax.broadcasted_iota(jnp.int32, (tile, 128), 1)
    for c in range(columns):
        own_rows = slice(c * tile, (c + 1) * tile)
        total = jnp.sum(low[own_rows, :], axis=1, keepdims=True)
        inverse = 1.0 / total
        attended = (acc[own_rows, :] * inverse).astype(BF16)
        out[own_rows, :] = attended
        delta = jnp.sum(mine[1, own_rows, :].astype(F32) * attended.astype(F32), axis=1, keepdims=True)
        both = jnp.where(lane == 0, top[own_rows, :] + jnp.log2(total), delta).T
        stats[c:c + 1, :] = both[0:1]
        stats[4 + c:5 + c, :] = both[1:2]
        top[own_rows, :] = jnp.broadcast_to(delta, (tile, 128))
        low[own_rows, :] = jnp.broadcast_to(inverse * scale, (tile, 128))
        acc[own_rows, :] = jnp.zeros((tile, 128), F32)

    def query_step(at, ours, tiles):
        for place, c, t in zip(at, ours, tiles):
            ds = s_all[place] * (w_all[place] - wide(top[rows(c), :]))
            acc[rows(c), :] += dot(ds.astype(BF16), near[0, rows(t), :], NN)

    for_groups(columns, lists, query_step)
    grad_q[...] = (acc[:columns * tile, :] * low[:columns * tile, :]).astype(BF16)


def for_turns(columns, lists, run):
    ends = [lists[places(columns) - columns + c] for c in range(columns)]

    def step(i, carry):
        subs = []
        for j in range(TURN):
            at = TURN * i + j
            column = sum([(at >= end).astype(jnp.int32) for end in ends[:-1]], jnp.int32(0))
            subs.append((column, [lists[SUB * at + p] for p in range(SUB)]))
        run(i, subs)
        return carry

    lax.fori_loop(0, (ends[-1] + TURN - 1) // TURN, step, 0)


def key_kernel(columns, tile, scale, lists, *refs):
    own, slots, sets = refs[:4], refs[4:SLOTS + 6], refs[SLOTS + 6:SLOTS + 9]
    grad_k, grad_v, near, mine, logs, deltas, k_acc, v_acc, sems = refs[SLOTS + 9:SLOTS + 18]
    probs, scores = refs[SLOTS + 18:SLOTS + 18 + TURN], refs[SLOTS + 18 + TURN:]
    copies = fetch(own, slots, near, mine, sems)
    spare = pl.ds(SLOTS * columns * tile, tile)
    near[:, spare] = jnp.zeros((2, tile, near.shape[2]), BF16)
    for slot in range(SLOTS):
        first = 8 * (slot // 3)
        logs[slot * columns:(slot + 1) * columns, :] = sets[slot % 3][first:first + columns, :]
        deltas[slot * columns:(slot + 1) * columns, :] = sets[slot % 3][first + 4:first + 4 + columns, :]
    logs[SLOTS * columns:, :] = jnp.full((5, tile), 1e30, F32)
    deltas[SLOTS * columns:, :] = jnp.zeros((5, tile), F32)
    k_acc[...] = jnp.zeros(k_acc.shape, F32)
    v_acc[...] = jnp.zeros(v_acc.shape, F32)
    for copy in copies:
        copy.wait()
    unit = scale * math.log2(math.e)

    def rows(index):
        return pl.ds(pl.multiple_of(index * tile, tile), tile)

    def stacked(which, tiles):
        return jnp.concatenate([near[which, rows(t), :] for t in tiles], 0)

    def step(i, subs):
        for j, (c, tiles) in enumerate(subs):
            k, v = mine[0, rows(c), :], mine[1, rows(c), :]
            for n, t in enumerate(tiles):
                part = slice(n * tile, (n + 1) * tile)
                p = jnp.exp2(dot(k, near[0, rows(t), :], NT) * unit - logs[pl.ds(t, 1), :])
                probs[j][:, part] = p.astype(BF16)
                w = dot(v, near[1, rows(t), :], NT) - deltas[pl.ds(t, 1), :]
                scores[j][:, part] = (p * w).astype(BF16)
            v_acc[rows(c), :] += dot(probs[j][...], stacked(1, tiles), NN)
            k_acc[rows(c), :] += dot(scores[j][...], stacked(0, tiles), NN)

    for_turns(columns, lists, step)
    grad_k[...] = (k_acc[...] * scale).astype(BF16)
    grad_v[...] = v_acc[...].astype(BF16)


def ring(axis, step):
    count = lax.axis_size(axis)
    return [(i, (i + step) % count) for i in range(count)]


def pair_up(axis, first):
    count = lax.axis_size(axis)
    to = list(range(count))
    for i in range(first, count - 1, 2):
        to[i], to[i + 1] = i + 1, i
    return list(enumerate(to))


def moves():
    return ring(ROWS, 1), ring(ROWS, -1), pair_up(TM, 0), pair_up(TM, 1)


def spread_small(x):
    before, after, near, far = moves()
    frames = jnp.concatenate([x, lax.ppermute(x, TM, near), lax.ppermute(x, TM, far)], 0)
    return [frames, lax.ppermute(frames, ROWS, before), lax.ppermute(frames, ROWS, after)]


def then(first, *values):
    return lax.optimization_barrier((first, *values))


ANY = pl.BlockSpec(memory_space=pl.ANY)
VMEM = pl.BlockSpec(memory_space=pltpu.VMEM)
HBM = pl.BlockSpec(memory_space=pltpu.HBM)
SMEM = pl.BlockSpec(memory_space=pltpu.SMEM)
PARAMS = pltpu.CompilerParams(vmem_limit_bytes=52 * 2**20)


def query_call(columns, lists, q, k, v, g, near_kv, scale):
    tokens, width = q.shape
    tile = tokens // columns
    field = jax.ShapeDtypeStruct((tokens, width), BF16)
    total = pltpu.VMEM(((columns + 1) * tile, width), F32)
    squares = pltpu.VMEM((list_size(columns) - 18, tile, tile), F32)
    return pl.pallas_call(
        lambda *refs: query_kernel(columns, tile, scale, *refs),
        out_shape=(field, field, jax.ShapeDtypeStruct((8, tile), F32)),
        in_specs=[SMEM] + [HBM] * 4 + [ANY] * (SLOTS + 2),
        out_specs=(VMEM, VMEM, VMEM),
        scratch_shapes=[
            pltpu.VMEM((2, SLOTS * tokens, width), BF16),
            pltpu.VMEM((2, tokens + tile, width), BF16),
            squares, squares,
            total, total, total,
            pltpu.SemaphoreType.DMA((SLOTS + 6,)),
        ],
        compiler_params=PARAMS,
        cost_estimate=pl.CostEstimate(
            flops=32 * 5 * 2 * tile * tile * width, bytes_accessed=8 * tokens * width, transcendentals=32 * tile * tile
        ),
        name="query_side",
    )(lists, k, v, q, g, *near_kv)


def key_call(columns, lists, q, k, v, g, near_qg, near_stats, scale):
    tokens, width = q.shape
    tile = tokens // columns
    field = jax.ShapeDtypeStruct((tokens, width), BF16)
    total = pltpu.VMEM((tokens, width), F32)
    return pl.pallas_call(
        lambda *refs: key_kernel(columns, tile, scale, *refs),
        out_shape=(field, field),
        in_specs=[SMEM] + [HBM] * 4 + [ANY] * (SLOTS + 2) + [VMEM] * 3,
        out_specs=(VMEM, VMEM),
        scratch_shapes=[
            pltpu.VMEM((2, SLOTS * tokens + tile, width), BF16),
            pltpu.VMEM((2, tokens, width), BF16),
            *[pltpu.VMEM((SLOTS * columns + 5, tile), F32)] * 2,
            total, total,
            pltpu.SemaphoreType.DMA((SLOTS + 6,)),
            *[pltpu.VMEM((tile, SUB * tile), BF16)] * (2 * TURN),
        ],
        compiler_params=PARAMS,
        cost_estimate=pl.CostEstimate(
            flops=32 * 4 * 2 * tile * tile * width, bytes_accessed=8 * tokens * width, transcendentals=32 * tile * tile
        ),
        name="key_side",
    )(lists, q, g, k, v, *near_qg, *near_stats)


def body(queries, keys, values, d_out, window_mask):
    columns, tile, width = queries.shape[2], queries.shape[4], queries.shape[5]
    tokens = columns * tile
    scale = width ** -0.5
    flat = lambda x: x.reshape(tokens, width)
    pair = jax.ShapeDtypeStruct((2, tokens, width), BF16)
    own = [flat(x) for x in (queries, keys, values, d_out)]
    kv, qg, pairs, subgroup_pairs = pl.pallas_call(
        lambda *refs: pack_kernel(columns, *refs),
        out_shape=(
            pair, pair,
            jax.ShapeDtypeStruct((list_size(columns),), jnp.int32),
            jax.ShapeDtypeStruct((places(columns),), jnp.int32),
        ),
        in_specs=[SMEM] + [VMEM] * 4,
        out_specs=(VMEM, VMEM, SMEM, SMEM),
        name="pack",
    )(window_mask, *own)
    before, after, near, far = moves()
    send = lax.ppermute
    kv_o = send(kv, TM, near)
    kv_up, kv_down = send(kv, ROWS, before), send(kv, ROWS, after)
    frame = lax.axis_index(TM)
    inner = (frame > 0) & (frame < lax.axis_size(TM) - 1)
    half = send(jnp.where(inner, kv[0], kv_o[1]), TM, ring(TM, 2))
    qg_o = send(qg, TM, near)
    qg_half = send(jnp.where(inner, qg[0], qg_o[1]), TM, ring(TM, 2))
    half, qg_next = then(half, qg)
    half_up, half_down = send(half, ROWS, before), send(half, ROWS, after)
    rest = send(half, TM, near)
    kv_ou, kv_od = send(kv_up, TM, near), send(kv_down, TM, near)
    qg_up, qg_down = send(qg_next, ROWS, before), send(qg_next, ROWS, after)
    qg_half, half_up, half_down = then(qg_half, half_up, half_down)
    rest_up, rest_down = send(half_up, TM, near), send(half_down, TM, near)
    qg_half_up, qg_half_down = send(qg_half, ROWS, before), send(qg_half, ROWS, after)
    near_kv = [kv_up, kv_down, kv_o, kv_ou, kv_od, rest, half, rest_up, half_up, rest_down, half_down]
    attended, grad_q, stats = query_call(columns, pairs, *own, near_kv, scale)
    stats, qg_half, qg_up, qg_down, qg_half_up, qg_half_down = then(
        stats, qg_half, qg_up, qg_down, qg_half_up, qg_half_down
    )
    near_stats = spread_small(stats)
    qg_ou, qg_od = send(qg_up, TM, near), send(qg_down, TM, near)
    qg_rest, qg_rest_up, qg_rest_down = [send(x, TM, near) for x in (qg_half, qg_half_up, qg_half_down)]
    near_qg = [
        qg_up, qg_down, qg_o, qg_ou, qg_od, qg_rest, qg_half, qg_rest_up, qg_half_up, qg_rest_down, qg_half_down
    ]
    grad_k, grad_v = key_call(columns, subgroup_pairs, *own, near_qg, near_stats, scale)
    return tuple(x.reshape(queries.shape) for x in (attended, grad_q, grad_k, grad_v))


def solution(mesh):
    field = P(TM, ROWS, None, "heads", None, None)
    return jax.shard_map(
        body,
        mesh=mesh,
        in_specs=(field, field, field, field, P(TM, ROWS, None, "heads", None)),
        out_specs=(field, field, field, field),
        check_vma=False,
    )
```

```python
import math

import jax
import jax.numpy as jnp
from jax import lax
from jax.experimental import pallas as pl
from jax.experimental.pallas import tpu as pltpu
from jax.sharding import PartitionSpec as P

TM, ROWS = "tm", "rows"
F32, BF16 = jnp.float32, jnp.bfloat16
SLOTS = 9
ROOM = 32
GROUP = 14
SUB = 3
TURN = 3
ROW_STEPS = (0, -1, 1)
NT = (((1,), (1,)), ((), ()))
NN = (((1,), (0,)), ((), ()))


def dot(left, right, dims):
    return lax.dot_general(left, right, dims, preferred_element_type=F32)


def find_pairs(mask, lists, columns):
    near = 1 - 2 * lax.rem(lax.axis_index(TM), 2)
    frame_steps = (0, near, -near)
    n = jnp.int32(0)
    for slot in range(SLOTS):
        dt, dr = frame_steps[slot // 3], ROW_STEPS[slot % 3]
        for c in range(columns):
            for other in range(max(c - 1, 0), min(c + 2, columns)):
                lists[n] = ROOM * c + slot * columns + other
                n = n + mask[0, 0, c, 0, 9 * (dt + 1) + 3 * (dr + 1) + other - c + 1]
    for extra in range(GROUP - 1):
        lists[n + extra] = ROOM * columns
    lists[list_size(columns) - 1] = (n + GROUP - 1) // GROUP


def list_size(columns):
    return 27 * columns + GROUP


def find_subgroups(mask, lists, columns):
    near = 1 - 2 * lax.rem(lax.axis_index(TM), 2)
    frame_steps = (0, near, -near)
    n = jnp.int32(0)
    for c in range(columns):
        for slot in range(SLOTS):
            dt, dr = frame_steps[slot // 3], ROW_STEPS[slot % 3]
            for other in range(max(c - 1, 0), min(c + 2, columns)):
                lists[n] = slot * columns + other
                n = n + mask[0, 0, c, 0, 9 * (dt + 1) + 3 * (dr + 1) + other - c + 1]
        for extra in range(SUB - 1):
            lists[n + extra] = SLOTS * columns
        end = (n + SUB - 1) // SUB
        lists[places(columns) - columns + c] = end
        n = end * SUB
    for extra in range(SUB * (TURN - 1)):
        lists[n + extra] = SLOTS * columns


def subgroups(columns):
    most = sum(-(-9 * (min(c + 2, columns) - max(c - 1, 0)) // SUB) for c in range(columns))
    return -(-most // TURN) * TURN


def places(columns):
    return (subgroups(columns) + TURN) * SUB + columns


def pack_kernel(columns, mask, q, k, v, g, kv, qg, pairs, subgroup_pairs):
    kv[0], kv[1], qg[0], qg[1] = k[...], v[...], q[...], g[...]
    find_pairs(mask, pairs, columns)
    find_subgroups(mask, subgroup_pairs, columns)


def fetch(own, slots, near, mine, sems):
    tokens = own[0].shape[0]
    copies = []
    for i in range(4):
        to = near if i < 2 else mine
        copies.append(pltpu.make_async_copy(own[i], to.at[i % 2, pl.ds(0, tokens)], sems.at[i]))
    for s in range(1, SLOTS):
        at = pl.ds(s * tokens, tokens)
        halves = len(slots) - SLOTS + 1
        if s <= len(slots) - 2 * halves:
            copies.append(pltpu.make_async_copy(slots[s - 1], near.at[:, at], sems.at[s + 3]))
        else:
            for i in range(2):
                n = 2 * s + i - SLOTS + halves - 1
                copies.append(pltpu.make_async_copy(slots[n], near.at[i, at], sems.at[n + 4]))
    for copy in copies:
        copy.start()
    return copies


def for_groups(columns, lists, run):
    def step(i, carry):
        at = [GROUP * i + j for j in range(GROUP)]
        entries = [lists[place] for place in at]
        run(at, [entry // ROOM for entry in entries], [lax.rem(entry, ROOM) for entry in entries])
        return carry

    lax.fori_loop(0, lists[list_size(columns) - 1], step, 0)


def query_kernel(columns, tile, scale, lists, *refs):
    own, slots = refs[:4], refs[4:SLOTS + 6]
    out, grad_q, stats = refs[SLOTS + 6:SLOTS + 9]
    near, mine, s_all, w_all, top, low, acc, sems = refs[SLOTS + 9:]
    copies = fetch(own, slots, near, mine, sems)
    unit = scale * math.log2(math.e)
    top[...] = jnp.full(top.shape, -jnp.inf, F32)
    low[...] = jnp.zeros(low.shape, F32)
    acc[...] = jnp.zeros(acc.shape, F32)
    for copy in copies:
        copy.wait()

    def rows(index):
        return pl.ds(pl.multiple_of(index * tile, tile), tile)

    def wide(x):
        return jnp.concatenate([x, x], 1)

    def score_step(at, ours, tiles):
        for place, c, t in zip(at, ours, tiles):
            s = dot(mine[0, rows(c), :], near[0, rows(t), :], NT) * unit
            s_all[place] = s
            top[rows(c), :] = jnp.maximum(top[rows(c), :], jnp.maximum(s[:, :128], s[:, 128:]))

    for_groups(columns, lists, score_step)
    for c in range(columns):
        own_rows = slice(c * tile, (c + 1) * tile)
        peak = jnp.max(top[own_rows, :], axis=1, keepdims=True)
        top[own_rows, :] = jnp.broadcast_to(peak, (tile, 128))

    def value_step(at, ours, tiles):
        for place, c, t in zip(at, ours, tiles):
            v = near[1, rows(t), :]
            e = jnp.exp2(s_all[place] - wide(top[rows(c), :]))
            s_all[place] = e
            w_all[place] = dot(mine[1, rows(c), :], v, NT)
            low[rows(c), :] += e[:, :128] + e[:, 128:]
            acc[rows(c), :] += dot(e.astype(BF16), v, NN)

    for_groups(columns, lists, value_step)
    lane = lax.broadcasted_iota(jnp.int32, (tile, 128), 1)
    for c in range(columns):
        own_rows = slice(c * tile, (c + 1) * tile)
        total = jnp.sum(low[own_rows, :], axis=1, keepdims=True)
        inverse = 1.0 / total
        attended = (acc[own_rows, :] * inverse).astype(BF16)
        out[own_rows, :] = attended
        delta = jnp.sum(mine[1, own_rows, :].astype(F32) * attended.astype(F32), axis=1, keepdims=True)
        both = jnp.where(lane == 0, top[own_rows, :] + jnp.log2(total), delta).T
        stats[c:c + 1, :] = both[0:1]
        stats[4 + c:5 + c, :] = both[1:2]
        top[own_rows, :] = jnp.broadcast_to(delta, (tile, 128))
        low[own_rows, :] = jnp.broadcast_to(inverse * scale, (tile, 128))
        acc[own_rows, :] = jnp.zeros((tile, 128), F32)

    def query_step(at, ours, tiles):
        for place, c, t in zip(at, ours, tiles):
            ds = s_all[place] * (w_all[place] - wide(top[rows(c), :]))
            acc[rows(c), :] += dot(ds.astype(BF16), near[0, rows(t), :], NN)

    for_groups(columns, lists, query_step)
    grad_q[...] = (acc[:columns * tile, :] * low[:columns * tile, :]).astype(BF16)


def for_turns(columns, lists, run):
    ends = [lists[places(columns) - columns + c] for c in range(columns)]

    def step(i, carry):
        subs = []
        for j in range(TURN):
            at = TURN * i + j
            column = sum([(at >= end).astype(jnp.int32) for end in ends[:-1]], jnp.int32(0))
            subs.append((column, [lists[SUB * at + p] for p in range(SUB)]))
        run(i, subs)
        return carry

    lax.fori_loop(0, (ends[-1] + TURN - 1) // TURN, step, 0)


def key_kernel(columns, tile, scale, lists, *refs):
    own, slots, sets = refs[:4], refs[4:SLOTS + 6], refs[SLOTS + 6:SLOTS + 9]
    grad_k, grad_v, near, mine, logs, deltas, k_acc, v_acc, sems = refs[SLOTS + 9:SLOTS + 18]
    probs, scores = refs[SLOTS + 18:SLOTS + 18 + TURN], refs[SLOTS + 18 + TURN:]
    copies = fetch(own, slots, near, mine, sems)
    spare = pl.ds(SLOTS * columns * tile, tile)
    near[:, spare] = jnp.zeros((2, tile, near.shape[2]), BF16)
    for slot in range(SLOTS):
        first = 8 * (slot // 3)
        logs[slot * columns:(slot + 1) * columns, :] = sets[slot % 3][first:first + columns, :]
        deltas[slot * columns:(slot + 1) * columns, :] = sets[slot % 3][first + 4:first + 4 + columns, :]
    logs[SLOTS * columns:, :] = jnp.full((5, tile), 1e30, F32)
    deltas[SLOTS * columns:, :] = jnp.zeros((5, tile), F32)
    k_acc[...] = jnp.zeros(k_acc.shape, F32)
    v_acc[...] = jnp.zeros(v_acc.shape, F32)
    for copy in copies:
        copy.wait()
    unit = scale * math.log2(math.e)

    def rows(index):
        return pl.ds(pl.multiple_of(index * tile, tile), tile)

    def stacked(which, tiles):
        return jnp.concatenate([near[which, rows(t), :] for t in tiles], 0)

    def step(i, subs):
        for j, (c, tiles) in enumerate(subs):
            k, v = mine[0, rows(c), :], mine[1, rows(c), :]
            for n, t in enumerate(tiles):
                part = slice(n * tile, (n + 1) * tile)
                p = jnp.exp2(dot(k, near[0, rows(t), :], NT) * unit - logs[pl.ds(t, 1), :])
                probs[j][:, part] = p.astype(BF16)
                w = dot(v, near[1, rows(t), :], NT) - deltas[pl.ds(t, 1), :]
                scores[j][:, part] = (p * w).astype(BF16)
            v_acc[rows(c), :] += dot(probs[j][...], stacked(1, tiles), NN)
            k_acc[rows(c), :] += dot(scores[j][...], stacked(0, tiles), NN)

    for_turns(columns, lists, step)
    grad_k[...] = (k_acc[...] * scale).astype(BF16)
    grad_v[...] = v_acc[...].astype(BF16)


def ring(axis, step):
    count = lax.axis_size(axis)
    return [(i, (i + step) % count) for i in range(count)]


def pair_up(axis, first):
    count = lax.axis_size(axis)
    to = list(range(count))
    for i in range(first, count - 1, 2):
        to[i], to[i + 1] = i + 1, i
    return list(enumerate(to))


def moves():
    return ring(ROWS, 1), ring(ROWS, -1), pair_up(TM, 0), pair_up(TM, 1)


def spread_small(x):
    before, after, near, far = moves()
    frames = jnp.concatenate([x, lax.ppermute(x, TM, near), lax.ppermute(x, TM, far)], 0)
    return [frames, lax.ppermute(frames, ROWS, before), lax.ppermute(frames, ROWS, after)]


def then(first, *values):
    return lax.optimization_barrier((first, *values))


ANY = pl.BlockSpec(memory_space=pl.ANY)
VMEM = pl.BlockSpec(memory_space=pltpu.VMEM)
HBM = pl.BlockSpec(memory_space=pltpu.HBM)
SMEM = pl.BlockSpec(memory_space=pltpu.SMEM)
PARAMS = pltpu.CompilerParams(vmem_limit_bytes=52 * 2**20)


def query_call(columns, lists, q, k, v, g, near_kv, scale):
    tokens, width = q.shape
    tile = tokens // columns
    field = jax.ShapeDtypeStruct((tokens, width), BF16)
    total = pltpu.VMEM(((columns + 1) * tile, width), F32)
    squares = pltpu.VMEM((list_size(columns) - 18, tile, tile), F32)
    return pl.pallas_call(
        lambda *refs: query_kernel(columns, tile, scale, *refs),
        out_shape=(field, field, jax.ShapeDtypeStruct((8, tile), F32)),
        in_specs=[SMEM] + [HBM] * 4 + [ANY] * (SLOTS + 2),
        out_specs=(VMEM, VMEM, VMEM),
        scratch_shapes=[
            pltpu.VMEM((2, SLOTS * tokens, width), BF16),
            pltpu.VMEM((2, tokens + tile, width), BF16),
            squares, squares,
            total, total, total,
            pltpu.SemaphoreType.DMA((SLOTS + 6,)),
        ],
        compiler_params=PARAMS,
        cost_estimate=pl.CostEstimate(
            flops=32 * 5 * 2 * tile * tile * width, bytes_accessed=8 * tokens * width, transcendentals=32 * tile * tile
        ),
        name="query_side",
    )(lists, k, v, q, g, *near_kv)


def key_call(columns, lists, q, k, v, g, near_qg, near_stats, scale):
    tokens, width = q.shape
    tile = tokens // columns
    field = jax.ShapeDtypeStruct((tokens, width), BF16)
    total = pltpu.VMEM((tokens, width), F32)
    return pl.pallas_call(
        lambda *refs: key_kernel(columns, tile, scale, *refs),
        out_shape=(field, field),
        in_specs=[SMEM] + [HBM] * 4 + [ANY] * (SLOTS + 2) + [VMEM] * 3,
        out_specs=(VMEM, VMEM),
        scratch_shapes=[
            pltpu.VMEM((2, SLOTS * tokens + tile, width), BF16),
            pltpu.VMEM((2, tokens, width), BF16),
            *[pltpu.VMEM((SLOTS * columns + 5, tile), F32)] * 2,
            total, total,
            pltpu.SemaphoreType.DMA((SLOTS + 6,)),
            *[pltpu.VMEM((tile, SUB * tile), BF16)] * (2 * TURN),
        ],
        compiler_params=pltpu.CompilerParams(vmem_limit_bytes=24 * 2**20),
        cost_estimate=pl.CostEstimate(
            flops=32 * 4 * 2 * tile * tile * width, bytes_accessed=8 * tokens * width, transcendentals=32 * tile * tile
        ),
        name="key_side",
    )(lists, q, g, k, v, *near_qg, *near_stats)


def body(queries, keys, values, d_out, window_mask):
    columns, tile, width = queries.shape[2], queries.shape[4], queries.shape[5]
    tokens = columns * tile
    scale = width ** -0.5
    flat = lambda x: x.reshape(tokens, width)
    pair = jax.ShapeDtypeStruct((2, tokens, width), BF16)
    own = [flat(x) for x in (queries, keys, values, d_out)]
    kv, qg, pairs, subgroup_pairs = pl.pallas_call(
        lambda *refs: pack_kernel(columns, *refs),
        out_shape=(
            pair, pair,
            jax.ShapeDtypeStruct((list_size(columns),), jnp.int32),
            jax.ShapeDtypeStruct((places(columns),), jnp.int32),
        ),
        in_specs=[SMEM] + [VMEM] * 4,
        out_specs=(VMEM, VMEM, SMEM, SMEM),
        name="pack",
    )(window_mask, *own)
    before, after, near, far = moves()
    send = lax.ppermute
    kv_o = send(kv, TM, near)
    kv_up, kv_down = send(kv, ROWS, before), send(kv, ROWS, after)
    frame = lax.axis_index(TM)
    inner = (frame > 0) & (frame < lax.axis_size(TM) - 1)
    half = send(jnp.where(inner, kv[0], kv_o[1]), TM, ring(TM, 2))
    qg_o = send(qg, TM, near)
    qg_half = send(jnp.where(inner, qg[0], qg_o[1]), TM, ring(TM, 2))
    half, qg_next = then(half, qg)
    half_up, half_down = send(half, ROWS, before), send(half, ROWS, after)
    rest = send(half, TM, near)
    kv_ou, kv_od = send(kv_up, TM, near), send(kv_down, TM, near)
    qg_up, qg_down = send(qg_next, ROWS, before), send(qg_next, ROWS, after)
    qg_half, half_up, half_down = then(qg_half, half_up, half_down)
    rest_up, rest_down = send(half_up, TM, near), send(half_down, TM, near)
    qg_half_up, qg_half_down = send(qg_half, ROWS, before), send(qg_half, ROWS, after)
    near_kv = [kv_up, kv_down, kv_o, kv_ou, kv_od, rest, half, rest_up, half_up, rest_down, half_down]
    attended, grad_q, stats = query_call(columns, pairs, *own, near_kv, scale)
    stats, qg_half, qg_up, qg_down, qg_half_up, qg_half_down = then(
        stats, qg_half, qg_up, qg_down, qg_half_up, qg_half_down
    )
    near_stats = spread_small(stats)
    qg_ou, qg_od = send(qg_up, TM, near), send(qg_down, TM, near)
    qg_rest, qg_rest_up, qg_rest_down = [send(x, TM, near) for x in (qg_half, qg_half_up, qg_half_down)]
    near_qg = [
        qg_up, qg_down, qg_o, qg_ou, qg_od, qg_rest, qg_half, qg_rest_up, qg_half_up, qg_rest_down, qg_half_down
    ]
    grad_k, grad_v = key_call(columns, subgroup_pairs, *own, near_qg, near_stats, scale)
    return tuple(x.reshape(queries.shape) for x in (attended, grad_q, grad_k, grad_v))


def solution(mesh):
    field = P(TM, ROWS, None, "heads", None, None)
    return jax.shard_map(
        body,
        mesh=mesh,
        in_specs=(field, field, field, field, P(TM, ROWS, None, "heads", None)),
        out_specs=(field, field, field, field),
        check_vma=False,
    )
```

```python
import math

import jax
import jax.numpy as jnp
from jax import lax
from jax.experimental import pallas as pl
from jax.experimental.pallas import tpu as pltpu
from jax.sharding import PartitionSpec as P

TM, ROWS = "tm", "rows"
F32, BF16 = jnp.float32, jnp.bfloat16
SLOTS = 9
ROOM = 32
GROUP = 14
SUB = 3
TURN = 3
ROW_STEPS = (0, -1, 1)
NT = (((1,), (1,)), ((), ()))
NN = (((1,), (0,)), ((), ()))


def dot(left, right, dims):
    return lax.dot_general(left, right, dims, preferred_element_type=F32)


def find_pairs(mask, lists, columns):
    near = 1 - 2 * lax.rem(lax.axis_index(TM), 2)
    frame_steps = (0, near, -near)
    n = jnp.int32(0)
    for slot in range(SLOTS):
        dt, dr = frame_steps[slot // 3], ROW_STEPS[slot % 3]
        for c in range(columns):
            for other in range(max(c - 1, 0), min(c + 2, columns)):
                lists[n] = ROOM * c + slot * columns + other
                n = n + mask[0, 0, c, 0, 9 * (dt + 1) + 3 * (dr + 1) + other - c + 1]
    for extra in range(GROUP - 1):
        lists[n + extra] = ROOM * columns
    lists[list_size(columns) - 1] = (n + GROUP - 1) // GROUP


def list_size(columns):
    return 27 * columns + GROUP


def find_subgroups(mask, lists, columns):
    near = 1 - 2 * lax.rem(lax.axis_index(TM), 2)
    frame_steps = (0, near, -near)
    n = jnp.int32(0)
    for c in range(columns):
        for slot in range(SLOTS):
            dt, dr = frame_steps[slot // 3], ROW_STEPS[slot % 3]
            for other in range(max(c - 1, 0), min(c + 2, columns)):
                lists[n] = slot * columns + other
                n = n + mask[0, 0, c, 0, 9 * (dt + 1) + 3 * (dr + 1) + other - c + 1]
        for extra in range(SUB - 1):
            lists[n + extra] = SLOTS * columns
        end = (n + SUB - 1) // SUB
        lists[places(columns) - columns + c] = end
        n = end * SUB
    for extra in range(SUB * (TURN - 1)):
        lists[n + extra] = SLOTS * columns


def subgroups(columns):
    most = sum(-(-9 * (min(c + 2, columns) - max(c - 1, 0)) // SUB) for c in range(columns))
    return -(-most // TURN) * TURN


def places(columns):
    return (subgroups(columns) + TURN) * SUB + columns


def pack_kernel(columns, mask, q, k, v, g, kv, qg, pairs, subgroup_pairs):
    kv[0], kv[1], qg[0], qg[1] = k[...], v[...], q[...], g[...]
    find_pairs(mask, pairs, columns)
    find_subgroups(mask, subgroup_pairs, columns)


def fetch(own, slots, near, mine, sems):
    tokens = own[0].shape[0]
    copies = []
    for i in range(4):
        to = near if i < 2 else mine
        copies.append(pltpu.make_async_copy(own[i], to.at[i % 2, pl.ds(0, tokens)], sems.at[i]))
    for s in range(1, SLOTS):
        at = pl.ds(s * tokens, tokens)
        halves = len(slots) - SLOTS + 1
        if s <= len(slots) - 2 * halves:
            copies.append(pltpu.make_async_copy(slots[s - 1], near.at[:, at], sems.at[s + 3]))
        else:
            for i in range(2):
                n = 2 * s + i - SLOTS + halves - 1
                copies.append(pltpu.make_async_copy(slots[n], near.at[i, at], sems.at[n + 4]))
    for copy in copies:
        copy.start()
    return copies


def for_groups(columns, lists, run):
    def step(i, carry):
        at = [GROUP * i + j for j in range(GROUP)]
        entries = [lists[place] for place in at]
        run(at, [entry // ROOM for entry in entries], [lax.rem(entry, ROOM) for entry in entries])
        return carry

    lax.fori_loop(0, lists[list_size(columns) - 1], step, 0)


def query_kernel(columns, tile, scale, lists, *refs):
    own, slots = refs[:4], refs[4:SLOTS + 6]
    out, grad_q, stats = refs[SLOTS + 6:SLOTS + 9]
    near, mine, s_all, w_all, top, low, acc, sems = refs[SLOTS + 9:]
    copies = fetch(own, slots, near, mine, sems)
    unit = scale * math.log2(math.e)
    top[...] = jnp.full(top.shape, -jnp.inf, F32)
    low[...] = jnp.zeros(low.shape, F32)
    acc[...] = jnp.zeros(acc.shape, F32)
    for copy in copies:
        copy.wait()

    def rows(index):
        return pl.ds(pl.multiple_of(index * tile, tile), tile)

    def wide(x):
        return jnp.concatenate([x, x], 1)

    def score_step(at, ours, tiles):
        for place, c, t in zip(at, ours, tiles):
            s = dot(mine[0, rows(c), :], near[0, rows(t), :], NT) * unit
            s_all[place] = s
            top[rows(c), :] = jnp.maximum(top[rows(c), :], jnp.maximum(s[:, :128], s[:, 128:]))

    for_groups(columns, lists, score_step)
    for c in range(columns):
        own_rows = slice(c * tile, (c + 1) * tile)
        peak = jnp.max(top[own_rows, :], axis=1, keepdims=True)
        top[own_rows, :] = jnp.broadcast_to(peak, (tile, 128))

    def value_step(at, ours, tiles):
        for place, c, t in zip(at, ours, tiles):
            v = near[1, rows(t), :]
            e = jnp.exp2(s_all[place] - wide(top[rows(c), :]))
            s_all[place] = e
            w_all[place] = dot(mine[1, rows(c), :], v, NT)
            low[rows(c), :] += e[:, :128] + e[:, 128:]
            acc[rows(c), :] += dot(e.astype(BF16), v, NN)

    for_groups(columns, lists, value_step)
    lane = lax.broadcasted_iota(jnp.int32, (tile, 128), 1)
    for c in range(columns):
        own_rows = slice(c * tile, (c + 1) * tile)
        total = jnp.sum(low[own_rows, :], axis=1, keepdims=True)
        inverse = 1.0 / total
        attended = (acc[own_rows, :] * inverse).astype(BF16)
        out[own_rows, :] = attended
        delta = jnp.sum(mine[1, own_rows, :].astype(F32) * attended.astype(F32), axis=1, keepdims=True)
        both = jnp.where(lane == 0, top[own_rows, :] + jnp.log2(total), delta).T
        stats[c:c + 1, :] = both[0:1]
        stats[4 + c:5 + c, :] = both[1:2]
        top[own_rows, :] = jnp.broadcast_to(delta, (tile, 128))
        low[own_rows, :] = jnp.broadcast_to(inverse * scale, (tile, 128))
        acc[own_rows, :] = jnp.zeros((tile, 128), F32)

    def query_step(at, ours, tiles):
        for place, c, t in zip(at, ours, tiles):
            ds = s_all[place] * (w_all[place] - wide(top[rows(c), :]))
            acc[rows(c), :] += dot(ds.astype(BF16), near[0, rows(t), :], NN)

    for_groups(columns, lists, query_step)
    grad_q[...] = (acc[:columns * tile, :] * low[:columns * tile, :]).astype(BF16)


def for_turns(columns, lists, run):
    ends = [lists[places(columns) - columns + c] for c in range(columns)]

    def step(i, carry):
        subs = []
        for j in range(TURN):
            at = TURN * i + j
            column = sum([(at >= end).astype(jnp.int32) for end in ends[:-1]], jnp.int32(0))
            subs.append((column, [lists[SUB * at + p] for p in range(SUB)]))
        run(i, subs)
        return carry

    lax.fori_loop(0, (ends[-1] + TURN - 1) // TURN, step, 0)


def key_kernel(columns, tile, scale, lists, *refs):
    own, slots, sets = refs[:4], refs[4:SLOTS + 6], refs[SLOTS + 6:SLOTS + 9]
    grad_k, grad_v, near, mine, logs, deltas, k_acc, v_acc, sems = refs[SLOTS + 9:SLOTS + 18]
    probs, scores = refs[SLOTS + 18:SLOTS + 18 + TURN], refs[SLOTS + 18 + TURN:]
    copies = fetch(own, slots, near, mine, sems)
    spare = pl.ds(SLOTS * columns * tile, tile)
    near[:, spare] = jnp.zeros((2, tile, near.shape[2]), BF16)
    for slot in range(SLOTS):
        first = 8 * (slot // 3)
        logs[slot * columns:(slot + 1) * columns, :] = sets[slot % 3][first:first + columns, :]
        deltas[slot * columns:(slot + 1) * columns, :] = sets[slot % 3][first + 4:first + 4 + columns, :]
    logs[SLOTS * columns:, :] = jnp.full((5, tile), 1e30, F32)
    deltas[SLOTS * columns:, :] = jnp.zeros((5, tile), F32)
    k_acc[...] = jnp.zeros(k_acc.shape, F32)
    v_acc[...] = jnp.zeros(v_acc.shape, F32)
    for copy in copies:
        copy.wait()
    unit = scale * math.log2(math.e)

    def rows(index):
        return pl.ds(pl.multiple_of(index * tile, tile), tile)

    def stacked(which, tiles):
        return jnp.concatenate([near[which, rows(t), :] for t in tiles], 0)

    def step(i, subs):
        for j, (c, tiles) in enumerate(subs):
            k, v = mine[0, rows(c), :], mine[1, rows(c), :]
            for n, t in enumerate(tiles):
                part = slice(n * tile, (n + 1) * tile)
                p = jnp.exp2(dot(k, near[0, rows(t), :], NT) * unit - logs[pl.ds(t, 1), :])
                probs[j][:, part] = p.astype(BF16)
                w = dot(v, near[1, rows(t), :], NT) - deltas[pl.ds(t, 1), :]
                scores[j][:, part] = (p * w).astype(BF16)
            v_acc[rows(c), :] += dot(probs[j][...], stacked(1, tiles), NN)
            k_acc[rows(c), :] += dot(scores[j][...], stacked(0, tiles), NN)

    for_turns(columns, lists, step)
    grad_k[...] = (k_acc[...] * scale).astype(BF16)
    grad_v[...] = v_acc[...].astype(BF16)


def ring(axis, step):
    count = lax.axis_size(axis)
    return [(i, (i + step) % count) for i in range(count)]


def pair_up(axis, first):
    count = lax.axis_size(axis)
    to = list(range(count))
    for i in range(first, count - 1, 2):
        to[i], to[i + 1] = i + 1, i
    return list(enumerate(to))


def moves():
    return ring(ROWS, 1), ring(ROWS, -1), pair_up(TM, 0), pair_up(TM, 1)


def spread_small(x):
    before, after, near, far = moves()
    frames = jnp.concatenate([x, lax.ppermute(x, TM, near), lax.ppermute(x, TM, far)], 0)
    return [frames, lax.ppermute(frames, ROWS, before), lax.ppermute(frames, ROWS, after)]


def then(first, *values):
    return lax.optimization_barrier((first, *values))


ANY = pl.BlockSpec(memory_space=pl.ANY)
VMEM = pl.BlockSpec(memory_space=pltpu.VMEM)
HBM = pl.BlockSpec(memory_space=pltpu.HBM)
SMEM = pl.BlockSpec(memory_space=pltpu.SMEM)
PARAMS = pltpu.CompilerParams(vmem_limit_bytes=44 * 2**20)


def query_call(columns, lists, q, k, v, g, near_kv, scale):
    tokens, width = q.shape
    tile = tokens // columns
    field = jax.ShapeDtypeStruct((tokens, width), BF16)
    total = pltpu.VMEM(((columns + 1) * tile, width), F32)
    squares = pltpu.VMEM((list_size(columns) - 25, tile, tile), F32)
    return pl.pallas_call(
        lambda *refs: query_kernel(columns, tile, scale, *refs),
        out_shape=(field, field, jax.ShapeDtypeStruct((8, tile), F32)),
        in_specs=[SMEM] + [HBM] * 4 + [ANY] * (SLOTS + 2),
        out_specs=(VMEM, VMEM, VMEM),
        scratch_shapes=[
            pltpu.VMEM((2, SLOTS * tokens, width), BF16),
            pltpu.VMEM((2, tokens + tile, width), BF16),
            squares, squares,
            total, total, total,
            pltpu.SemaphoreType.DMA((SLOTS + 6,)),
        ],
        compiler_params=PARAMS,
        cost_estimate=pl.CostEstimate(
            flops=32 * 5 * 2 * tile * tile * width, bytes_accessed=8 * tokens * width, transcendentals=32 * tile * tile
        ),
        name="query_side",
    )(lists, k, v, q, g, *near_kv)


def key_call(columns, lists, q, k, v, g, near_qg, near_stats, scale):
    tokens, width = q.shape
    tile = tokens // columns
    field = jax.ShapeDtypeStruct((tokens, width), BF16)
    total = pltpu.VMEM((tokens, width), F32)
    return pl.pallas_call(
        lambda *refs: key_kernel(columns, tile, scale, *refs),
        out_shape=(field, field),
        in_specs=[SMEM] + [HBM] * 4 + [ANY] * (SLOTS + 2) + [VMEM] * 3,
        out_specs=(VMEM, VMEM),
        scratch_shapes=[
            pltpu.VMEM((2, SLOTS * tokens + tile, width), BF16),
            pltpu.VMEM((2, tokens, width), BF16),
            *[pltpu.VMEM((SLOTS * columns + 5, tile), F32)] * 2,
            total, total,
            pltpu.SemaphoreType.DMA((SLOTS + 6,)),
            *[pltpu.VMEM((tile, SUB * tile), BF16)] * (2 * TURN),
        ],
        compiler_params=pltpu.CompilerParams(vmem_limit_bytes=24 * 2**20),
        cost_estimate=pl.CostEstimate(
            flops=32 * 4 * 2 * tile * tile * width, bytes_accessed=8 * tokens * width, transcendentals=32 * tile * tile
        ),
        name="key_side",
    )(lists, q, g, k, v, *near_qg, *near_stats)


def body(queries, keys, values, d_out, window_mask):
    columns, tile, width = queries.shape[2], queries.shape[4], queries.shape[5]
    tokens = columns * tile
    scale = width ** -0.5
    flat = lambda x: x.reshape(tokens, width)
    pair = jax.ShapeDtypeStruct((2, tokens, width), BF16)
    own = [flat(x) for x in (queries, keys, values, d_out)]
    kv, qg, pairs, subgroup_pairs = pl.pallas_call(
        lambda *refs: pack_kernel(columns, *refs),
        out_shape=(
            pair, pair,
            jax.ShapeDtypeStruct((list_size(columns),), jnp.int32),
            jax.ShapeDtypeStruct((places(columns),), jnp.int32),
        ),
        in_specs=[SMEM] + [VMEM] * 4,
        out_specs=(VMEM, VMEM, SMEM, SMEM),
        name="pack",
    )(window_mask, *own)
    before, after, near, far = moves()
    send = lax.ppermute
    kv_o = send(kv, TM, near)
    kv_up, kv_down = send(kv, ROWS, before), send(kv, ROWS, after)
    frame = lax.axis_index(TM)
    inner = (frame > 0) & (frame < lax.axis_size(TM) - 1)
    half = send(jnp.where(inner, kv[0], kv_o[1]), TM, ring(TM, 2))
    qg_o = send(qg, TM, near)
    qg_half = send(jnp.where(inner, qg[0], qg_o[1]), TM, ring(TM, 2))
    half, qg_next = then(half, qg)
    half_up, half_down = send(half, ROWS, before), send(half, ROWS, after)
    rest = send(half, TM, near)
    kv_ou, kv_od = send(kv_up, TM, near), send(kv_down, TM, near)
    qg_up, qg_down = send(qg_next, ROWS, before), send(qg_next, ROWS, after)
    qg_half, half_up, half_down = then(qg_half, half_up, half_down)
    rest_up, rest_down = send(half_up, TM, near), send(half_down, TM, near)
    qg_half_up, qg_half_down = send(qg_half, ROWS, before), send(qg_half, ROWS, after)
    near_kv = [kv_up, kv_down, kv_o, kv_ou, kv_od, rest, half, rest_up, half_up, rest_down, half_down]
    attended, grad_q, stats = query_call(columns, pairs, *own, near_kv, scale)
    stats, qg_half, qg_up, qg_down, qg_half_up, qg_half_down = then(
        stats, qg_half, qg_up, qg_down, qg_half_up, qg_half_down
    )
    near_stats = spread_small(stats)
    qg_ou, qg_od = send(qg_up, TM, near), send(qg_down, TM, near)
    qg_rest, qg_rest_up, qg_rest_down = [send(x, TM, near) for x in (qg_half, qg_half_up, qg_half_down)]
    near_qg = [
        qg_up, qg_down, qg_o, qg_ou, qg_od, qg_rest, qg_half, qg_rest_up, qg_half_up, qg_rest_down, qg_half_down
    ]
    grad_k, grad_v = key_call(columns, subgroup_pairs, *own, near_qg, near_stats, scale)
    return tuple(x.reshape(queries.shape) for x in (attended, grad_q, grad_k, grad_v))


def solution(mesh):
    field = P(TM, ROWS, None, "heads", None, None)
    return jax.shard_map(
        body,
        mesh=mesh,
        in_specs=(field, field, field, field, P(TM, ROWS, None, "heads", None)),
        out_specs=(field, field, field, field),
        check_vma=False,
    )
```
